32 devices in a mesh: context: 8 (over z, y), tensor: 4 (over x, core).
Axes of the slice: x: 2, y: 2, z: 4, core: 2. Of those that a mesh axis runs over, the one named last changes fastest.
Arguments:
- layer_input: bfloat16 [4096, 1024], P('context', 'tensor'), may hold values from -6 to 6
- value_proj: bfloat16 [1024, 2048], P(None, 'tensor'), may hold values from -0.1875 to 0.1875
- conv_taps: float32 [4, 2048], P(None, 'tensor'), may hold values from -3 to 3
- conv_pre: bfloat16 [4096, 2048], P('context', 'tensor'), may hold values from -6 to 6
- state_in: bfloat16 [4096, 128], P('context'), may hold values from -6 to 6
- state_out: bfloat16 [4096, 128], P('context'), may hold values from -0.5 to 0.5
- step_size: float32 [32, 4096], P('tensor', 'context'), may hold values from 0 to 1
- log_decay: float32 [32, 4096], P('tensor', 'context'), may hold values from -2 to 0
- skip_gain: float32 [32], P('tensor'), may hold values from 0.5 to 2
- grad_out: bfloat16 [4096, 2048], P('context', 'tensor'), may hold values from -6 to 6
Outputs:
- grad_input: bfloat16 [4096, 1024], P('context', 'tensor')
- grad_value_proj: float32 [1024, 2048], P('context', 'tensor')
The draws below stay inside these ranges and needn't reach their ends.
All inputs are finite; a program needn't handle non-finite values.
Results may differ from the reference program's by a relative error of at most 0.0059.
Values may be sent and summed in bfloat16 or wider, within the bound.
No kernel may reach another device: no remote copies, remote signals or barrier semaphores. Data moves between devices by JAX's collectives and lax.ppermute only.
A program may use at most 64 MiB of HBM per device.

```python
import math
import jax
import jax.numpy as jnp
from jax import lax

D = 1024
HEADS = 32
HEAD_DIM = 64
STATE = 128
CONV = 4
BLOCK = 256
TOK_DEV = 512
INNER = 2048
TOKEN_SPAN = 4096


def head_rates(key, fast_share, chain_share):
    chooser_key, chain_key, device_key, fast_key = jax.random.split(key, 4)
    chooser = jax.random.uniform(chooser_key, (HEADS,))
    chain_rate = jnp.exp(jax.random.uniform(chain_key, (HEADS,), minval=math.log(0.15), maxval=math.log(0.8))) * 2.3 / TOKEN_SPAN
    device_rate = jnp.exp(jax.random.uniform(device_key, (HEADS,), minval=math.log(0.25), maxval=0.0)) * 2.3 / TOK_DEV
    fast_rate = 2.3 / jnp.exp(jax.random.uniform(fast_key, (HEADS,), minval=math.log(30.0), maxval=math.log(50.0)))
    slow_rate = jnp.where(chooser < fast_share + chain_share, chain_rate, device_rate)
    return jnp.where(chooser < fast_share, fast_rate, slow_rate)


def draw_log_decay(key, part):
    rates = head_rates(key, 0.35, 0.45)
    key = jax.random.fold_in(key, 11)
    angle_seed_handle, coarse_seed_handle, spike_seed_handle, magnitude_seed_handle = jax.random.split(key, 4)
    places = jnp.arange(TOKEN_SPAN, dtype=jnp.float32)
    phase = jax.random.uniform(angle_seed_handle, (), minval=0.0, maxval=2.0 * math.pi)
    swing = jnp.exp(0.8 * jnp.sin(2.0 * math.pi * 3.0 * places / TOKEN_SPAN + phase))
    rough = jnp.exp(jax.random.uniform(coarse_seed_handle, (HEADS, TOKEN_SPAN), minval=math.log(0.5), maxval=math.log(2.0)))
    placement_indices = jax.random.randint(spike_seed_handle, (2,), 0, TOKEN_SPAN)
    struck = jnp.any(jnp.arange(TOKEN_SPAN)[None, :] == placement_indices[:, None], axis=0)
    amount = jax.random.uniform(magnitude_seed_handle, (HEADS, TOKEN_SPAN), minval=0.22, maxval=0.51)
    return -(rates[:, None] * swing[None, :] * rough) - jnp.where(struck[None, :], amount, 0.0)


def draw_step_size(key, part):
    rates = head_rates(key, 0.35, 0.45)
    key = jax.random.fold_in(key, 12)
    jitter = jax.random.uniform(key, (HEADS, TOKEN_SPAN), minval=0.5, maxval=1.5)
    return jnp.sqrt(rates)[:, None] * jitter


def strengthened(drawn, rng, source, target, shards_of, factor):
    def block_of(dim):
        return (jnp.arange(drawn.shape[dim]) // (drawn.shape[dim] // shards_of)).reshape((-1,) + (1,) * (drawn.ndim - 1 - dim))

    first = jax.random.permutation(rng, shards_of)[block_of(target)]
    other_side = (block_of(target) + shards_of // 2) % shards_of
    return jnp.where((block_of(source) == first) | (block_of(source) == other_side), factor * drawn, drawn)


def block_levels(own_key, extent, cuts, least, largest):
    factor_of = 1.0
    for axis_at, parts in cuts:
        steps = jax.random.uniform(jax.random.fold_in(jax.random.fold_in(own_key, 6), axis_at), (parts,), jnp.float32, least / len(cuts), largest / len(cuts))
        factor_of = factor_of * jnp.repeat(jnp.exp(steps), extent[axis_at] // parts).reshape((-1,) + (1,) * (len(extent) - 1 - axis_at))
    return factor_of


def gaussian(key, dims, scale, reach, cuts=(), kind=jnp.bfloat16):
    drawn = scale * jax.random.normal(key, dims, jnp.float32)
    if cuts:
        drawn = drawn * block_levels(key, dims, cuts, -0.22, 0.18)
    return jnp.clip(drawn, -reach, reach).astype(kind)


def heavy_noise(own_key, dims, width, bound, shards, heavy, kind=jnp.bfloat16):
    array = width * jax.random.normal(own_key, dims, jnp.float32)
    if shards:
        array = array * block_levels(own_key, dims, shards, -0.22, 0.18)
    return jnp.clip(strengthened(array, jax.random.fold_in(own_key, 3), *heavy), -bound, bound).astype(kind)


def setup_inputs(seed: int = 0) -> dict:
    key_of = jax.random.split(jax.random.key(seed), 11)
    layer_input = heavy_noise(key_of[0], (TOKEN_SPAN, D), 1.0, 6.0, ((0, 8), (1, 4)), (0, 1, 8, 2.0))
    value_proj = gaussian(key_of[1], (D, INNER), D ** -0.5, 0.1875, ((1, 4),))
    conv_taps = gaussian(key_of[2], (CONV, INNER), CONV ** -0.5, 3.0, ((1, 4),), jnp.float32)
    conv_pre = gaussian(key_of[3], (TOKEN_SPAN, INNER), 1.0, 6.0, ((0, 8), (1, 4)))
    state_in = gaussian(key_of[4], (TOKEN_SPAN, STATE), 1.0, 6.0, ((0, 8),))
    state_out = gaussian(key_of[5], (TOKEN_SPAN, STATE), STATE ** -0.5, 0.5, ((0, 8),))
    step_size = draw_step_size(jax.random.fold_in(key_of[10], 71), 0)
    log_decay = draw_log_decay(jax.random.fold_in(key_of[10], 71), 0)
    skip_gain = jnp.clip(0.5 + 1.5 * jax.random.uniform(key_of[8], (HEADS,), jnp.float32) ** block_levels(key_of[8], (HEADS,), ((0, 4),), -0.2, 0.2), 0.5, 2.0)
    grad_out = gaussian(key_of[9], (TOKEN_SPAN, INNER), 1.0, 6.0, ((0, 8), (1, 4)))
    return dict(layer_input=layer_input, value_proj=value_proj, conv_taps=conv_taps, conv_pre=conv_pre, state_in=state_in, state_out=state_out, step_size=step_size, log_decay=log_decay, skip_gain=skip_gain, grad_out=grad_out)


precise = lax.Precision.HIGHEST

def silu_slope(values):
    sigmoid_value = jax.nn.sigmoid(values)
    return sigmoid_value * (1.0 + values * (1.0 - sigmoid_value))

def block_grads(carried, input_blk, output_blk, grad_blk, step_blk, decay_blk, skip_gain):
    running_total = jnp.cumsum(decay_blk, axis=1)
    closing = running_total[:, -1:]
    length = input_blk.shape[0]
    scores = jnp.dot(input_blk, output_blk.T, preferred_element_type=jnp.float32)
    spread = running_total[:, None, :] - running_total[:, :, None]
    upper_mask = jnp.arange(length)[None, :] >= jnp.arange(length)[:, None]
    damping = jnp.where(upper_mask[None], jnp.exp(jnp.minimum(spread, 0.0)), 0.0)
    weights = (scores[None] * damping).astype(jnp.bfloat16)
    grad_float = grad_blk.astype(jnp.float32)
    within = jnp.einsum('hts,shp->thp', weights.astype(jnp.float32), grad_float, precision=precise)
    carried_low = lax.optimization_barrier(carried.astype(jnp.bfloat16)).astype(jnp.float32)
    beyond = jnp.einsum('hpn,tn->thp', carried_low, input_blk.astype(jnp.float32), precision=precise)
    beyond = beyond * jnp.exp(closing - running_total).T[:, :, None]
    grad_x = step_blk.T[:, :, None] * (within + beyond) + skip_gain[None, :, None] * grad_float
    weighted = (grad_float * jnp.exp(running_total).T[:, :, None]).astype(jnp.bfloat16)
    weighted = lax.optimization_barrier(weighted).astype(jnp.float32)
    block_state = jnp.einsum('shp,sn->hpn', weighted, output_blk.astype(jnp.float32), precision=precise)
    return (grad_x, jnp.exp(closing)[:, :, None] * carried + block_state)

def reference(layer_input, value_proj, conv_taps, conv_pre, state_in, state_out, step_size, log_decay, skip_gain, grad_out):
    block_count = TOKEN_SPAN // BLOCK
    block_parts = (state_in.reshape(block_count, BLOCK, STATE), state_out.reshape(block_count, BLOCK, STATE), grad_out.reshape(block_count, BLOCK, HEADS, HEAD_DIM), conv_pre.reshape(block_count, BLOCK, INNER), step_size.reshape(HEADS, block_count, BLOCK).transpose(1, 0, 2), log_decay.reshape(HEADS, block_count, BLOCK).transpose(1, 0, 2))

    def block_step(carried, pieces):
        grad_x, carried = block_grads(carried, pieces[0], pieces[1], pieces[2], pieces[4], pieces[5], skip_gain)
        slope = silu_slope(pieces[3].astype(jnp.float32))
        grad_conv = (grad_x.reshape(BLOCK, INNER) * slope).astype(jnp.bfloat16)
        return (carried, grad_conv)
    empty_state = jnp.zeros((HEADS, HEAD_DIM, STATE), jnp.float32)
    grad_conv = lax.scan(block_step, empty_state, block_parts, reverse=True)[1].reshape(TOKEN_SPAN, INNER)
    extended = jnp.concatenate([grad_conv.astype(jnp.float32), jnp.zeros((CONV - 1, INNER), jnp.float32)], axis=0)
    summed = jnp.zeros((TOKEN_SPAN, INNER), jnp.float32)
    for offset in range(CONV):
        start_row = CONV - 1 - offset
        summed = summed + conv_taps[offset][None, :] * extended[start_row:start_row + TOKEN_SPAN]
    grad_proj = summed.astype(jnp.bfloat16)
    grad_input = jnp.dot(grad_proj, value_proj.T, preferred_element_type=jnp.float32).astype(jnp.bfloat16)
    grad_value_proj = jnp.dot(layer_input.T, grad_proj, preferred_element_type=jnp.float32) * (1.0 / math.sqrt(TOKEN_SPAN))
    return (grad_input, grad_value_proj)
```

```python
import functools
import math

import jax
import jax.numpy as jnp
from jax import lax
from jax.experimental import pallas as pl
from jax.experimental.pallas import tpu as pltpu
from jax.sharding import PartitionSpec as P

CONV = 4
BLOCK = 256
PAD = 16
ROW = 8
F32 = jnp.float32
BF16 = jnp.bfloat16
MIB = 1024 * 1024


def call(body, out_shapes, operands, scalars=0, hbm=0, idle=0, scratch=(), flops=0, moved=0, vmem=8):
    blocks = len(operands) - scalars - hbm - idle
    in_specs = [pl.BlockSpec(memory_space=pltpu.SMEM)] * scalars
    in_specs += [pl.BlockSpec(memory_space=pltpu.VMEM)] * blocks
    in_specs += [pl.BlockSpec(memory_space=pltpu.HBM)] * hbm
    in_specs += [pl.BlockSpec(memory_space=pl.ANY)] * idle
    kept = len(operands) - idle

    def run(*refs):
        body(*refs[:kept], *refs[len(operands) :])

    operands = list(operands)
    for index in range(scalars + blocks, scalars + blocks + hbm):
        operands[index] = pltpu.with_memory_space_constraint(operands[index], pltpu.HBM)
    return pl.pallas_call(
        run,
        out_shape=[jax.ShapeDtypeStruct(shape, kind) for shape, kind in out_shapes],
        in_specs=in_specs,
        out_specs=[pl.BlockSpec(memory_space=pltpu.VMEM)] * len(out_shapes),
        scratch_shapes=list(scratch),
        compiler_params=pltpu.CompilerParams(vmem_limit_bytes=vmem * MIB),
        cost_estimate=pl.CostEstimate(flops=flops, bytes_accessed=moved, transcendentals=0),
    )(*operands)


def radices(count, largest):
    found = []
    while count > 1:
        radix = next(r for r in range(min(largest, count), count + 1) if count % r == 0)
        found.append(radix)
        count //= radix
    return found


def partner(digit, radix, hop):
    if radix & (radix - 1) == 0:
        return digit ^ hop
    return (digit + hop) % radix


def origin(digit, radix, hop):
    if radix & (radix - 1) == 0:
        return digit ^ hop
    return (digit + radix - hop) % radix


def swap(value, axis, stride, radix, hop, back=False):
    count = lax.axis_size(axis)
    pairs = []
    for source in range(count):
        digit = source // stride % radix
        target = source + (partner(digit, radix, hop) - digit) * stride
        if not back or target < source:
            pairs.append((source, target))
    return lax.ppermute(value, axis, pairs)


def dot(a, b, contract):
    return lax.dot_general(a, b, ((contract[:1], contract[1:]), ((), ())), preferred_element_type=F32)


def spread_heads(heads, width):
    lane = lax.broadcasted_iota(jnp.int32, (heads, width), 1)
    head = lax.broadcasted_iota(jnp.int32, (heads, width), 0)
    return (lane // (width // heads) == head).astype(F32)


def spread_scalars(ref, heads, width):
    head = lax.broadcasted_iota(jnp.int32, (1, width), 1) // (width // heads)
    wide = jnp.zeros((1, width), F32)
    for index in range(heads):
        wide = jnp.where(head == index, ref[index], wide)
    return wide


def widen(per_head, spreader):
    high = per_head.astype(BF16).astype(F32)
    parts = jnp.concatenate([high, per_head - high], axis=0).astype(BF16)
    twice = jnp.concatenate([spreader, spreader], axis=0).astype(BF16)
    return dot(parts, twice, (0, 0))


def split(values):
    high = values.astype(BF16).astype(F32)
    middle = (values - high).astype(BF16).astype(F32)
    return high, middle, values - high - middle


def running(decay_blk):
    heads, length = decay_blk.shape
    row = lax.broadcasted_iota(jnp.int32, (length, length), 0)
    column = lax.broadcasted_iota(jnp.int32, (length, length), 1)
    parts = jnp.concatenate(split(decay_blk), axis=0).astype(BF16)
    sums = dot(parts, (row <= column).astype(F32).astype(BF16), (1, 0))
    return sums[:heads] + (sums[heads : 2 * heads] + sums[2 * heads :])


def pack_state(ref, state, decay_row):
    rows = state.shape[0]
    ref[:rows, :] = state.astype(BF16)
    high, middle, low = split(decay_row)
    place = lax.broadcasted_iota(jnp.int32, (PAD, decay_row.shape[1]), 0)
    packed = jnp.where(place == 0, high, jnp.where(place == 1, middle, jnp.where(place == 2, low, 0.0)))
    ref[rows:, :] = packed.astype(BF16)


def unpack_state(ref):
    rows = ref.shape[0] - PAD
    return ref[:rows, :].astype(F32), jnp.sum(ref[rows:, :].astype(F32), axis=0, keepdims=True)


def later_sum(digit, places, states, decays):
    total = None
    span = jnp.zeros_like(decays[0])
    for index, place in enumerate(places):
        between = jnp.zeros_like(decays[0])
        for other, other_place in enumerate(places):
            if other != index:
                inside = jnp.logical_and(other_place > digit, other_place < place)
                between = between + jnp.where(inside, decays[other], 0.0)
        weight = jnp.where(place > digit, jnp.exp(between), 0.0)
        total = weight * states[index] if total is None else total + weight * states[index]
        span = span + jnp.where(place > digit, decays[index], 0.0)
    return total, span


def state_body(heads, others, grad_hbm, output_hbm, decay_hbm, *refs):
    rest, refs = refs[:others], refs[others:]
    payload_ref, states_ref, grad_ref, output_ref, decay_ref = refs[:5]
    rest_out, sems = refs[5:-1], refs[-1]
    pairs = [(grad_hbm, grad_ref), (output_hbm, output_ref), (decay_hbm, decay_ref), *zip(rest, rest_out)]
    copies = [pltpu.make_async_copy(a, b, sems.at[index]) for index, (a, b) in enumerate(pairs)]
    firsts, later = copies[:3], copies[3:]
    for copy in firsts + later:
        copy.start()
    for copy in firsts:
        copy.wait()
    width = grad_ref.shape[1]
    count = grad_ref.shape[0] // BLOCK
    spreader = spread_heads(heads, width)
    states, spans = [], []
    for k in range(count):
        rows = slice(k * BLOCK, (k + 1) * BLOCK)
        cumulative = running(decay_ref[:, rows])
        spans.append(jnp.sum(spreader * cumulative[:, BLOCK - 1 :], axis=0, keepdims=True))
        weighted = (grad_ref[rows, :].astype(F32) * widen(jnp.exp(cumulative), spreader)).astype(BF16)
        states.append(dot(output_ref[rows, :], weighted, (0, 0)))
    total, span = states[-1], spans[-1]
    for k in reversed(range(count - 1)):
        total = states[k] + jnp.exp(spans[k]) * total
        span = span + spans[k]
    pack_state(payload_ref, total, span)
    for k in range(count):
        keep_state(states_ref.at[k], states[k], spans[k])
    for copy in later:
        copy.wait()


def keep_state(ref, state, span):
    rows = state.shape[0]
    ref[:rows, :] = state
    ref[rows:, :] = jnp.broadcast_to(span, (ROW, span.shape[1]))


def kept_state(ref):
    rows = ref.shape[0] - ROW
    return ref[:rows, :], ref[rows : rows + 1, :]


def merge_body(radix, stride, first, payload_ref, *refs):
    received = refs[: radix - 1]
    next_ref, held_out = refs[-2:]
    digit = lax.axis_index("context") // stride % radix
    pairs = [unpack_state(ref) for ref in (payload_ref, *received)]
    states, decays = [a for a, _ in pairs], [b for _, b in pairs]
    places = [origin(digit, radix, hop) for hop in range(radix)]
    whole, whole_span = later_sum(-1, places, states, decays)
    pack_state(next_ref, whole, whole_span)
    later, span = later_sum(digit, places[1:], states[1:], decays[1:])
    if not first:
        held, reach = kept_state(refs[radix - 1])
        later = held + jnp.exp(reach) * later
        span = reach + span
    keep_state(held_out, later, span)


def within_body(heads, skip_ref, *refs):
    input_ref, output_ref, grad_ref, step_ref, decay_ref, pre_ref, base_ref, coef_ref = refs
    for k in range(grad_ref.shape[0] // BLOCK):
        rows = slice(k * BLOCK, (k + 1) * BLOCK)
        within_block(
            heads,
            skip_ref,
            *(ref.at[rows, :] for ref in (input_ref, output_ref, grad_ref)),
            *(ref.at[:, rows] for ref in (step_ref, decay_ref)),
            *(ref.at[rows, :] for ref in (pre_ref, base_ref, coef_ref)),
        )


def within_block(heads, skip_ref, input_ref, output_ref, grad_ref, step_ref, decay_ref, pre_ref, base_ref, coef_ref):
    width = grad_ref.shape[1]
    head_width = width // heads
    group = max(1, 128 // head_width)
    half = BLOCK // 2
    spreader = spread_heads(heads, width)
    cumulative = running(decay_ref[...])
    across = cumulative.T
    scores = dot(input_ref[...], output_ref[...], (1, 1))
    step = step_ref[...]
    step_wide = widen(step, spreader)
    reach_wide = widen(step * jnp.exp(cumulative[:, BLOCK - 1 :] - cumulative), spreader)
    skip_wide = spread_scalars(skip_ref, heads, width)
    row = lax.broadcasted_iota(jnp.int32, (half, half), 0)
    column = lax.broadcasted_iota(jnp.int32, (half, half), 1)
    keep = column >= row
    lane = lax.broadcasted_iota(jnp.int32, (half, group * head_width), 1) // head_width

    def weigh(head, rows, columns, diagonal):
        spread = cumulative[head : head + 1, columns] - across[rows, head : head + 1]
        if diagonal:
            spread = jnp.where(keep, spread, -jnp.inf)
        return (scores[rows, columns] * jnp.exp(spread)).astype(BF16)

    first, second = slice(0, half), slice(half, BLOCK)
    for start in range(0, heads, group):
        channels = slice(start * head_width, (start + group) * head_width)
        grads = grad_ref[:, channels]
        upper = lower = None
        for member in range(group):
            head = start + member
            top = jnp.concatenate([weigh(head, first, first, True), weigh(head, first, second, False)], axis=1)
            one = dot(top, grads, (1, 0))
            two = dot(weigh(head, second, second, True), grads[half:, :], (1, 0))
            upper = one if upper is None else jnp.where(lane == member, one, upper)
            lower = two if lower is None else jnp.where(lane == member, two, lower)
        for rows, product in ((first, upper), (second, lower)):
            pre = pre_ref[rows, channels].astype(F32)
            gate = 1.0 / (1.0 + jnp.exp(-pre))
            slope = gate * (1.0 + pre * (1.0 - gate))
            direct = step_wide[rows, channels] * product + skip_wide[:, channels] * grads[rows, :].astype(F32)
            base_ref[rows, channels] = slope * direct
            coef_ref[rows, channels] = slope * reach_wide[rows, channels]


def turn_body(members, *refs):
    pieces, turned, ends_ref = refs[:members], refs[members : 2 * members], refs[-1]
    for hop in range(members):
        ends_ref[hop] = pieces[hop][pieces[hop].shape[0] - PAD :, :]
    for hop in range(members):
        turned[hop][...] = pieces[hop][...].T


def tail_body(radix, stride, first, members, chunk, *refs):
    received, refs = refs[: radix - 1], refs[radix - 1 :]
    if not first:
        held_ref, refs = refs[0], refs[1:]
    states_ref, base_ref, coef_ref, input_ref, taps_ref, ends_ref = refs[:6]
    layer_refs = refs[6 : 6 + members]
    keep_near, send_near, keep_far, send_far, grads_ref, conv_ref = refs[6 + members :]
    length, width = base_ref.shape
    place = lax.axis_index("context")
    digit = place // stride % radix
    pairs = [unpack_state(ref) for ref in received]
    places = [origin(digit, radix, hop) for hop in range(1, radix)]
    carry, _ = later_sum(digit, places, [a for a, _ in pairs], [b for _, b in pairs])
    if not first:
        held, reach = kept_state(held_ref)
        carry = held + jnp.exp(reach) * carry
    conv_ref[:PAD, :] = jnp.zeros((PAD, width), F32)
    conv_ref[PAD + length :, :] = jnp.zeros((PAD, width), F32)
    for k in reversed(range(length // BLOCK)):
        rows = slice(k * BLOCK, (k + 1) * BLOCK)
        product = dot(input_ref[rows, :], carry.astype(BF16), (1, 0))
        value = base_ref[rows, :] + coef_ref[rows, :] * product
        conv_ref[PAD + k * BLOCK : PAD + (k + 1) * BLOCK, :] = value.astype(BF16).astype(F32)
        if k:
            state, span = kept_state(states_ref.at[k])
            carry = state + jnp.exp(span) * carry
    total = None
    for offset in range(CONV):
        shift = CONV - 1 - offset
        term = taps_ref[offset : offset + 1, :] * conv_ref[shift : shift + PAD + length, :]
        total = term if total is None else total + term
    grads_ref[...] = total.astype(BF16)
    features = layer_refs[0].shape[0]
    per_piece = features // chunk
    me = lax.axis_index("tensor")
    half = width // 2

    def put(keep, send, same, index, value):
        @pl.when(same)
        def _():
            keep[index] = value

        @pl.when(jnp.logical_not(same))
        def _():
            send[index] = value.astype(BF16)

    for hop in range(members):
        source = origin(me, members, hop)
        product = dot(layer_refs[hop][...], grads_ref[PAD:, :], (1, 0)) + dot(ends_ref[hop], grads_ref[:PAD, :], (0, 0))
        for index in range(per_piece):
            number = source * per_piece + index
            rows = product[index * chunk : (index + 1) * chunk, :]
            put(keep_near, send_near, (number & 1) == (place & 1), number >> 1, rows[:, :half])
            put(keep_far, send_far, (number & 2) == (place & 2), (number & 1) + ((number >> 2) << 1), rows[:, half:])


def overlaps(index, high, sizes):
    start, found = 0, []
    for part, size in enumerate(sizes):
        first, last = max(start, index * high), min(start + size, (index + 1) * high)
        if first < last:
            found.append((part, slice(first - start, last - start), slice(first - index * high, last - index * high)))
        start += size
    return found


def share_body(members, sizes, grads_ref, proj_ref, *refs):
    keep_refs, send_refs = refs[: members // 2], refs[members // 2 :]
    high, features = keep_refs[0].shape
    for hop in range(members):
        goal = lax.axis_index("tensor") ^ hop
        block = proj_ref[pl.ds(pl.multiple_of(goal * features, features), features), :]
        share = dot(grads_ref[...], block, (1, 1))
        if hop % 2:
            for part, there, here in overlaps(hop // 2, high, sizes):
                send_refs[part][there, :] = share[here, :].astype(BF16)
        else:
            keep_refs[hop // 2][...] = share


def share_sum_body(count, sizes, *refs):
    keeps, arrivals, outs = refs[:count], refs[count : count + len(sizes)], refs[count + len(sizes) :]
    for index in range(count):
        out = outs[index // 2 + index % 2 * (count // 2)]
        for part, there, here in overlaps(index, out.shape[0], sizes):
            out[here, :] = (keeps[index][here, :] + arrivals[part][there, :].astype(F32)).astype(out.dtype)


def settle_body(share_ref, arrived_ref, head_ref, own_ref):
    head_ref[...] = share_ref[:PAD, :] + arrived_ref[:PAD, :].astype(F32)
    own_ref[...] = share_ref[PAD:, :] + arrived_ref[PAD:, :].astype(F32)


def end_body(scaling, keep_ref, got_ref, own_ref, ahead_ref, proj_out, input_out):
    proj_out[...] = (keep_ref[0] + got_ref[0].astype(F32)) * scaling
    rest = own_ref.shape[0] - PAD
    input_out[:rest, :] = own_ref[:rest, :].astype(BF16)
    input_out[rest:, :] = (own_ref[rest:, :] + ahead_ref[...]).astype(BF16)


def halve(bit, keep_ref, received_ref, keep_out, send_out):
    for index in range(keep_out.shape[0]):
        mine, other = 2 * index + bit, 2 * index + 1 - bit
        keep_out[index] = keep_ref[mine] + received_ref[mine].astype(F32)
        send_out[index] = (keep_ref[other] + received_ref[other].astype(F32)).astype(BF16)


def bit_of_place(shift):
    return (lax.axis_index("context") >> shift) & 1


def halve_body(shift, keep_ref, received_ref, keep_out, send_out):
    halve(bit_of_place(shift), keep_ref, received_ref, keep_out, send_out)


def halve_both_body(keep_near, got_near, keep_far, got_far, near_out, near_send, far_out, far_send):
    halve(bit_of_place(1), keep_near, got_near, near_out, near_send)
    halve(bit_of_place(0), keep_far, got_far, far_out, far_send)


def join_body(keep_near, got_near, keep_far, got_far, keep_out, send_out):
    bit = bit_of_place(2)
    half = keep_near.shape[2]
    halve(bit, keep_near, got_near, keep_out.at[:, :, :half], send_out.at[:, :, :half])
    halve(bit, keep_far, got_far, keep_out.at[:, :, half:], send_out.at[:, :, half:])


def local(
    layer_input,
    value_proj,
    conv_taps,
    conv_pre,
    state_in,
    state_out,
    step_size,
    log_decay,
    skip_gain,
    grad_out,
):
    length, width = grad_out.shape
    heads = step_size.shape[0]
    state_width = state_in.shape[1]
    count = length // BLOCK
    features = layer_input.shape[1]
    spans_of = lax.axis_size("context")
    members = lax.axis_size("tensor")

    layers = [layer_input]
    stride = members // 2
    while stride:
        layers += [swap(layer, "tensor", stride, 2, 1) for layer in layers]
        stride //= 2
    bits = members.bit_length() - 1
    layers = [layers[int(format(hop, f"0{bits}b")[::-1], 2)] for hop in range(members)]

    fetched = [grad_out, state_out, log_decay, state_in, step_size, conv_pre, conv_taps]
    payload, states, grad_here, output_here, decay_here, input_here, step_here, pre_here, taps_here = call(
        functools.partial(state_body, heads, len(fetched) - 3),
        [((state_width + PAD, width), BF16), ((count, state_width + ROW, width), F32)]
        + [(a.shape, a.dtype) for a in fetched],
        fetched,
        hbm=len(fetched),
        scratch=[pltpu.SemaphoreType.DMA((len(fetched),))],
        flops=2 * length * width * state_width,
        moved=2 * length * width,
        vmem=12,
    )

    base, coef = call(
        functools.partial(within_body, heads),
        [((length, width), F32), ((length, width), F32)],
        [skip_gain, input_here, output_here, grad_here, step_here, decay_here, pre_here],
        scalars=1,
        flops=64 * length * width * BLOCK * 8,
        moved=12 * length * width,
        vmem=16,
    )

    stages = radices(spans_of, 4)
    stride, held = 1, []
    for radix in stages:
        last = stride * radix == spans_of
        received = [swap(payload, "context", stride, radix, hop, last) for hop in range(1, radix)]
        if not last:
            payload, *held = call(
                functools.partial(merge_body, radix, stride, not held),
                [(payload.shape, BF16), ((state_width + ROW, width), F32)],
                [payload, *received, *held, base],
                idle=1,
            )
            stride *= radix

    *layers, ends = call(
        functools.partial(turn_body, members),
        [((features, length), BF16)] * members + [((members, PAD, features), BF16)],
        layers,
        moved=2 * members * features * length,
    )
    ends = lax.ppermute(ends, "context", [(i, i + 1) for i in range(spans_of - 1)])

    total_rows = members * features
    chunk = total_rows // spans_of
    scaling = 1.0 / math.sqrt(length * spans_of)
    split_shape = (spans_of // 2, chunk, width // 2)
    keep_near, send_near, keep_far, send_far, grads = call(
        functools.partial(tail_body, stages[-1], stride, not held, members, chunk),
        [(split_shape, F32), (split_shape, BF16), (split_shape, F32), (split_shape, BF16), ((PAD + length, width), BF16)],
        [*received, *held, states, base, coef, input_here, taps_here, ends, *layers],
        scratch=[pltpu.VMEM((length + 2 * PAD, width), F32)],
        flops=2 * length * width * total_rows,
        moved=16 * length * width,
        vmem=16,
    )

    got_near = swap(send_near, "context", 1, 2, 1)
    got_far = swap(send_far, "context", 2, 2, 1)

    quarter_shape = (spans_of // 4, chunk, width // 2)
    keep_near, send_near, keep_far, send_far = call(
        halve_both_body,
        [(quarter_shape, F32), (quarter_shape, BF16)] * 2,
        [keep_near, got_near, keep_far, got_far],
        moved=2 * total_rows * width,
        vmem=8,
    )
    got_near = swap(send_near, "context", 2, 2, 1)
    got_far = swap(send_far, "context", 1, 2, 1)
    half = members // 2
    high = PAD + length
    size = -(-half * high // (3 * PAD)) * PAD
    sizes = [min(size, half * high - start) for start in range(0, half * high, size)]
    shares = call(
        functools.partial(share_body, members, sizes),
        [((high, features), F32)] * half + [((size, features), BF16) for size in sizes],
        [grads, value_proj],
        flops=2 * length * width * total_rows,
        moved=8 * length * width,
        vmem=12,
    )
    stride = 1
    share, arrived = shares[:half], [swap(a, "tensor", stride, 2, 1) for a in shares[half:]]
    while half > 1:
        count, half = half, half // 2
        outs = call(
            functools.partial(share_sum_body, count, sizes),
            [((high, features), F32)] * half + [((high, features), BF16)] * half,
            [*share, *arrived],
            moved=4 * length * features,
        )
        stride *= 2
        sizes = [high] * half
        share, arrived = outs[:half], [swap(a, "tensor", stride, 2, 1) for a in outs[half:]]

    joined_shape = (spans_of // 8, chunk, width)
    keep, send = call(
        join_body,
        [(joined_shape, F32), (joined_shape, BF16)],
        [keep_near, got_near, keep_far, got_far],
        moved=total_rows * width,
        vmem=8,
    )
    got, shift = swap(send, "context", 4, 2, 1), 3
    while keep.shape[0] > 1:
        joined_shape = (keep.shape[0] // 2, chunk, width)
        keep, send = call(
            functools.partial(halve_body, shift),
            [(joined_shape, F32), (joined_shape, BF16)],
            [keep, got],
            moved=total_rows * width,
            vmem=8,
        )
        got = swap(send, "context", 1 << shift, 2, 1)
        shift += 1
    head, own = call(
        settle_body,
        [((PAD, features), F32), ((length, features), F32)],
        [*share, *arrived],
    )
    ahead = lax.ppermute(head, "context", [(i + 1, i) for i in range(spans_of - 1)])
    grad_value_proj, grad_input = call(
        functools.partial(end_body, scaling),
        [((chunk, width), F32), ((length, features), BF16)],
        [keep, got, own, ahead],
    )
    return (grad_input, grad_value_proj)


def solution(mesh):
    return jax.shard_map(
        local,
        mesh=mesh,
        in_specs=(
            P("context", "tensor"),
            P(None, "tensor"),
            P(None, "tensor"),
            P("context", "tensor"),
            P("context", None),
            P("context", None),
            P("tensor", "context"),
            P("tensor", "context"),
            P("tensor"),
            P("context", "tensor"),
        ),
        out_specs=(P("context", "tensor"), P("context", "tensor")),
        check_vma=False,
    )
```

```python
import functools
import math

import jax
import jax.numpy as jnp
from jax import lax
from jax.experimental import pallas as pl
from jax.experimental.pallas import tpu as pltpu
from jax.sharding import PartitionSpec as P

CONV = 4
BLOCK = 256
PAD = 16
ROW = 8
F32 = jnp.float32
BF16 = jnp.bfloat16
MIB = 1024 * 1024


def call(body, out_shapes, operands, scalars=0, hbm=0, idle=0, scratch=(), flops=0, moved=0, vmem=8):
    blocks = len(operands) - scalars - hbm - idle
    in_specs = [pl.BlockSpec(memory_space=pltpu.SMEM)] * scalars
    in_specs += [pl.BlockSpec(memory_space=pltpu.VMEM)] * blocks
    in_specs += [pl.BlockSpec(memory_space=pltpu.HBM)] * hbm
    in_specs += [pl.BlockSpec(memory_space=pl.ANY)] * idle
    kept = len(operands) - idle

    def run(*refs):
        body(*refs[:kept], *refs[len(operands) :])

    operands = list(operands)
    for index in range(scalars + blocks, scalars + blocks + hbm):
        operands[index] = pltpu.with_memory_space_constraint(operands[index], pltpu.HBM)
    return pl.pallas_call(
        run,
        out_shape=[jax.ShapeDtypeStruct(shape, kind) for shape, kind in out_shapes],
        in_specs=in_specs,
        out_specs=[pl.BlockSpec(memory_space=pltpu.VMEM)] * len(out_shapes),
        scratch_shapes=list(scratch),
        compiler_params=pltpu.CompilerParams(vmem_limit_bytes=vmem * MIB),
        cost_estimate=pl.CostEstimate(flops=flops, bytes_accessed=moved, transcendentals=0),
    )(*operands)


def radices(count, largest):
    found = []
    while count > 1:
        radix = next(r for r in range(min(largest, count), count + 1) if count % r == 0)
        found.append(radix)
        count //= radix
    return found


def partner(digit, radix, hop):
    if radix & (radix - 1) == 0:
        return digit ^ hop
    return (digit + hop) % radix


def origin(digit, radix, hop):
    if radix & (radix - 1) == 0:
        return digit ^ hop
    return (digit + radix - hop) % radix


def swap(value, axis, stride, radix, hop, back=False):
    count = lax.axis_size(axis)
    pairs = []
    for source in range(count):
        digit = source // stride % radix
        target = source + (partner(digit, radix, hop) - digit) * stride
        if not back or target < source:
            pairs.append((source, target))
    return lax.ppermute(value, axis, pairs)


def dot(a, b, contract):
    return lax.dot_general(a, b, ((contract[:1], contract[1:]), ((), ())), preferred_element_type=F32)


def spread_heads(heads, width):
    lane = lax.broadcasted_iota(jnp.int32, (heads, width), 1)
    head = lax.broadcasted_iota(jnp.int32, (heads, width), 0)
    return (lane // (width // heads) == head).astype(F32)


def spread_scalars(ref, heads, width):
    head = lax.broadcasted_iota(jnp.int32, (1, width), 1) // (width // heads)
    wide = jnp.zeros((1, width), F32)
    for index in range(heads):
        wide = jnp.where(head == index, ref[index], wide)
    return wide


def widen(per_head, spreader):
    high = per_head.astype(BF16).astype(F32)
    parts = jnp.concatenate([high, per_head - high], axis=0).astype(BF16)
    twice = jnp.concatenate([spreader, spreader], axis=0).astype(BF16)
    return dot(parts, twice, (0, 0))


def split(values):
    high = values.astype(BF16).astype(F32)
    middle = (values - high).astype(BF16).astype(F32)
    return high, middle, values - high - middle


def running(decay_blk):
    heads, length = decay_blk.shape
    row = lax.broadcasted_iota(jnp.int32, (length, length), 0)
    column = lax.broadcasted_iota(jnp.int32, (length, length), 1)
    parts = jnp.concatenate(split(decay_blk), axis=0).astype(BF16)
    sums = dot(parts, (row <= column).astype(F32).astype(BF16), (1, 0))
    return sums[:heads] + (sums[heads : 2 * heads] + sums[2 * heads :])


def pack_state(ref, state, decay_row):
    rows = state.shape[0]
    ref[:rows, :] = state.astype(BF16)
    high, middle, low = split(decay_row)
    place = lax.broadcasted_iota(jnp.int32, (PAD, decay_row.shape[1]), 0)
    packed = jnp.where(place == 0, high, jnp.where(place == 1, middle, jnp.where(place == 2, low, 0.0)))
    ref[rows:, :] = packed.astype(BF16)


def unpack_state(ref):
    rows = ref.shape[0] - PAD
    return ref[:rows, :].astype(F32), jnp.sum(ref[rows:, :].astype(F32), axis=0, keepdims=True)


def later_sum(digit, places, states, decays):
    total = None
    span = jnp.zeros_like(decays[0])
    for index, place in enumerate(places):
        between = jnp.zeros_like(decays[0])
        for other, other_place in enumerate(places):
            if other != index:
                inside = jnp.logical_and(other_place > digit, other_place < place)
                between = between + jnp.where(inside, decays[other], 0.0)
        weight = jnp.where(place > digit, jnp.exp(between), 0.0)
        total = weight * states[index] if total is None else total + weight * states[index]
        span = span + jnp.where(place > digit, decays[index], 0.0)
    return total, span


def state_body(heads, others, grad_hbm, output_hbm, decay_hbm, *refs):
    rest, refs = refs[:others], refs[others:]
    payload_ref, states_ref, grad_ref, output_ref, decay_ref = refs[:5]
    rest_out, sems = refs[5:-1], refs[-1]
    pairs = [(grad_hbm, grad_ref), (output_hbm, output_ref), (decay_hbm, decay_ref), *zip(rest, rest_out)]
    copies = [pltpu.make_async_copy(a, b, sems.at[index]) for index, (a, b) in enumerate(pairs)]
    firsts, later = copies[:3], copies[3:]
    for copy in firsts + later:
        copy.start()
    for copy in firsts:
        copy.wait()
    width = grad_ref.shape[1]
    count = grad_ref.shape[0] // BLOCK
    spreader = spread_heads(heads, width)
    states, spans = [], []
    for k in range(count):
        rows = slice(k * BLOCK, (k + 1) * BLOCK)
        cumulative = running(decay_ref[:, rows])
        spans.append(jnp.sum(spreader * cumulative[:, BLOCK - 1 :], axis=0, keepdims=True))
        weighted = (grad_ref[rows, :].astype(F32) * widen(jnp.exp(cumulative), spreader)).astype(BF16)
        states.append(dot(output_ref[rows, :], weighted, (0, 0)))
    total, span = states[-1], spans[-1]
    for k in reversed(range(count - 1)):
        total = states[k] + jnp.exp(spans[k]) * total
        span = span + spans[k]
    pack_state(payload_ref, total, span)
    for k in range(count):
        keep_state(states_ref.at[k], states[k], spans[k])
    for copy in later:
        copy.wait()


def keep_state(ref, state, span):
    rows = state.shape[0]
    ref[:rows, :] = state
    ref[rows:, :] = jnp.broadcast_to(span, (ROW, span.shape[1]))


def kept_state(ref):
    rows = ref.shape[0] - ROW
    return ref[:rows, :], ref[rows : rows + 1, :]


def merge_body(radix, stride, first, payload_ref, *refs):
    received = refs[: radix - 1]
    next_ref, held_out = refs[-2:]
    digit = lax.axis_index("context") // stride % radix
    pairs = [unpack_state(ref) for ref in (payload_ref, *received)]
    states, decays = [a for a, _ in pairs], [b for _, b in pairs]
    places = [origin(digit, radix, hop) for hop in range(radix)]
    whole, whole_span = later_sum(-1, places, states, decays)
    if next_ref.shape[0] > whole.shape[0]:
        pack_state(next_ref, whole, whole_span)
    else:
        next_ref[...] = whole.astype(BF16)
    later, span = later_sum(digit, places[1:], states[1:], decays[1:])
    if not first:
        held, reach = kept_state(refs[radix - 1])
        later = held + jnp.exp(reach) * later
        span = reach + span
    keep_state(held_out, later, span)


def within_body(heads, skip_ref, *refs):
    input_ref, output_ref, grad_ref, step_ref, decay_ref, pre_ref, base_ref, coef_ref = refs
    for k in range(grad_ref.shape[0] // BLOCK):
        rows = slice(k * BLOCK, (k + 1) * BLOCK)
        within_block(
            heads,
            skip_ref,
            *(ref.at[rows, :] for ref in (input_ref, output_ref, grad_ref)),
            *(ref.at[:, rows] for ref in (step_ref, decay_ref)),
            *(ref.at[rows, :] for ref in (pre_ref, base_ref, coef_ref)),
        )


def within_block(heads, skip_ref, input_ref, output_ref, grad_ref, step_ref, decay_ref, pre_ref, base_ref, coef_ref):
    width = grad_ref.shape[1]
    head_width = width // heads
    group = max(1, 128 // head_width)
    half = BLOCK // 2
    spreader = spread_heads(heads, width)
    cumulative = running(decay_ref[...])
    across = cumulative.T
    scores = dot(input_ref[...], output_ref[...], (1, 1))
    step = step_ref[...]
    step_wide = widen(step, spreader)
    reach_wide = widen(step * jnp.exp(cumulative[:, BLOCK - 1 :] - cumulative), spreader)
    skip_wide = spread_scalars(skip_ref, heads, width)
    row = lax.broadcasted_iota(jnp.int32, (half, half), 0)
    column = lax.broadcasted_iota(jnp.int32, (half, half), 1)
    keep = column >= row
    lane = lax.broadcasted_iota(jnp.int32, (half, group * head_width), 1) // head_width

    def weigh(head, rows, columns, diagonal):
        spread = cumulative[head : head + 1, columns] - across[rows, head : head + 1]
        if diagonal:
            spread = jnp.where(keep, spread, -jnp.inf)
        return (scores[rows, columns] * jnp.exp(spread)).astype(BF16)

    first, second = slice(0, half), slice(half, BLOCK)
    for start in range(0, heads, group):
        channels = slice(start * head_width, (start + group) * head_width)
        grads = grad_ref[:, channels]
        upper = lower = None
        for member in range(group):
            head = start + member
            top = jnp.concatenate([weigh(head, first, first, True), weigh(head, first, second, False)], axis=1)
            one = dot(top, grads, (1, 0))
            two = dot(weigh(head, second, second, True), grads[half:, :], (1, 0))
            upper = one if upper is None else jnp.where(lane == member, one, upper)
            lower = two if lower is None else jnp.where(lane == member, two, lower)
        for rows, product in ((first, upper), (second, lower)):
            pre = pre_ref[rows, channels].astype(F32)
            gate = 1.0 / (1.0 + jnp.exp(-pre))
            slope = gate * (1.0 + pre * (1.0 - gate))
            direct = step_wide[rows, channels] * product + skip_wide[:, channels] * grads[rows, :].astype(F32)
            base_ref[rows, channels] = slope * direct
            coef_ref[rows, channels] = slope * reach_wide[rows, channels]


def turn_body(members, *refs):
    pieces, turned, ends_ref = refs[:members], refs[members : 2 * members], refs[-1]
    for hop in range(members):
        ends_ref[hop] = pieces[hop][pieces[hop].shape[0] - PAD :, :]
    for hop in range(members):
        turned[hop][...] = pieces[hop][...].T


def tail_body(radix, stride, first, members, chunk, *refs):
    received, refs = refs[: radix - 1], refs[radix - 1 :]
    if not first:
        held_ref, refs = refs[0], refs[1:]
    states_ref, base_ref, coef_ref, input_ref, taps_ref, ends_ref = refs[:6]
    layer_refs = refs[6 : 6 + members]
    keep_near, send_near, keep_far, send_far, grads_ref, conv_ref = refs[6 + members :]
    length, width = base_ref.shape
    place = lax.axis_index("context")
    digit = place // stride % radix
    if radix == 2:
        carry = jnp.where(digit == 0, received[0][...].astype(F32), 0.0)
    else:
        pairs = [unpack_state(ref) for ref in received]
        places = [origin(digit, radix, hop) for hop in range(1, radix)]
        carry, _ = later_sum(digit, places, [a for a, _ in pairs], [b for _, b in pairs])
    if not first:
        held, reach = kept_state(held_ref)
        carry = held + jnp.exp(reach) * carry
    conv_ref[:PAD, :] = jnp.zeros((PAD, width), F32)
    conv_ref[PAD + length :, :] = jnp.zeros((PAD, width), F32)
    for k in reversed(range(length // BLOCK)):
        rows = slice(k * BLOCK, (k + 1) * BLOCK)
        product = dot(input_ref[rows, :], carry.astype(BF16), (1, 0))
        value = base_ref[rows, :] + coef_ref[rows, :] * product
        conv_ref[PAD + k * BLOCK : PAD + (k + 1) * BLOCK, :] = value.astype(BF16).astype(F32)
        if k:
            state, span = kept_state(states_ref.at[k])
            carry = state + jnp.exp(span) * carry
    total = None
    for offset in range(CONV):
        shift = CONV - 1 - offset
        term = taps_ref[offset : offset + 1, :] * conv_ref[shift : shift + PAD + length, :]
        total = term if total is None else total + term
    grads_ref[...] = total.astype(BF16)
    features = layer_refs[0].shape[0]
    per_piece = features // chunk
    me = lax.axis_index("tensor")
    half = width // 2

    def put(keep, send, bit, there, zero, one):
        mine = bit == 0
        keep[there] = jnp.where(mine, zero, one)
        send[there] = jnp.where(mine, one, zero).astype(BF16)

    near_bit, far_bit = place & 1, (place >> 1) & 1
    for start in range(0, members, 2):
        products = []
        for hop in (start, start + 1):
            ends = ends_ref[hop]
            products.append(dot(layer_refs[hop][...], grads_ref[PAD:, :], (1, 0)) + dot(ends, grads_ref[:PAD, :], (0, 0)))
        chunks = [[p[i * chunk : (i + 1) * chunk, :] for i in range(per_piece)] for p in products]
        sources = [origin(me, members, hop) for hop in (start, start + 1)]
        for source, parts in zip(sources, chunks):
            for i in range(0, per_piece, 2):
                zero, one = parts[i][:, :half], parts[i + 1][:, :half]
                put(keep_near, send_near, near_bit, (source * per_piece + i) >> 1, zero, one)
        if per_piece > 2:
            for source, parts in zip(sources, chunks):
                for i in range(per_piece):
                    if not i & 2:
                        number = source * per_piece + i
                        zero, one = parts[i][:, half:], parts[i + 2][:, half:]
                        put(keep_far, send_far, far_bit, (number & 1) + ((number >> 2) << 1), zero, one)
        else:
            swapped = (sources[0] & 1) ^ far_bit
            for i in range(per_piece):
                there = i + ((sources[0] >> 1) << 1)
                put(keep_far, send_far, swapped, there, chunks[0][i][:, half:], chunks[1][i][:, half:])


def overlaps(index, high, sizes):
    start, found = 0, []
    for part, size in enumerate(sizes):
        first, last = max(start, index * high), min(start + size, (index + 1) * high)
        if first < last:
            found.append((part, slice(first - start, last - start), slice(first - index * high, last - index * high)))
        start += size
    return found


def share_body(members, sizes, grads_ref, proj_ref, *refs):
    keep_refs, send_refs = refs[: members // 2], refs[members // 2 :]
    high, features = keep_refs[0].shape
    for hop in range(members):
        goal = lax.axis_index("tensor") ^ hop
        block = proj_ref[pl.ds(pl.multiple_of(goal * features, features), features), :]
        share = dot(grads_ref[...], block, (1, 1))
        if hop % 2:
            for part, there, here in overlaps(hop // 2, high, sizes):
                send_refs[part][there, :] = share[here, :].astype(BF16)
        else:
            keep_refs[hop // 2][...] = share


def share_sum_body(count, sizes, *refs):
    keeps, arrivals, outs = refs[:count], refs[count : count + len(sizes)], refs[count + len(sizes) :]
    for index in range(count):
        out = outs[index // 2 + index % 2 * (count // 2)]
        for part, there, here in overlaps(index, out.shape[0], sizes):
            out[here, :] = (keeps[index][here, :] + arrivals[part][there, :].astype(F32)).astype(out.dtype)


def settle_body(share_ref, arrived_ref, head_ref, own_ref):
    head_ref[...] = share_ref[:PAD, :] + arrived_ref[:PAD, :].astype(F32)
    own_ref[...] = share_ref[PAD:, :] + arrived_ref[PAD:, :].astype(F32)


def input_end_body(own_ref, ahead_ref, out_ref):
    rest = own_ref.shape[0] - PAD
    out_ref[:rest, :] = own_ref[:rest, :].astype(BF16)
    out_ref[rest:, :] = (own_ref[rest:, :] + ahead_ref[...]).astype(BF16)


def proj_end_body(scaling, keep_ref, got_ref, out_ref):
    out_ref[...] = (keep_ref[0] + got_ref[0].astype(F32)) * scaling


def halve(bit, keep_ref, received_ref, keep_out, send_out):
    for index in range(keep_out.shape[0]):
        mine, other = 2 * index + bit, 2 * index + 1 - bit
        keep_out[index] = keep_ref[mine] + received_ref[mine].astype(F32)
        send_out[index] = (keep_ref[other] + received_ref[other].astype(F32)).astype(BF16)


def bit_of_place(shift):
    return (lax.axis_index("context") >> shift) & 1


def halve_body(shift, keep_ref, received_ref, keep_out, send_out):
    halve(bit_of_place(shift), keep_ref, received_ref, keep_out, send_out)


def halve_both_body(keep_near, got_near, keep_far, got_far, near_out, near_send, far_out, far_send):
    halve(bit_of_place(1), keep_near, got_near, near_out, near_send)
    halve(bit_of_place(0), keep_far, got_far, far_out, far_send)


def join_body(keep_near, got_near, keep_far, got_far, keep_out, send_out):
    bit = bit_of_place(2)
    half = keep_near.shape[2]
    halve(bit, keep_near, got_near, keep_out.at[:, :, :half], send_out.at[:, :, :half])
    halve(bit, keep_far, got_far, keep_out.at[:, :, half:], send_out.at[:, :, half:])


def local(
    layer_input,
    value_proj,
    conv_taps,
    conv_pre,
    state_in,
    state_out,
    step_size,
    log_decay,
    skip_gain,
    grad_out,
):
    length, width = grad_out.shape
    heads = step_size.shape[0]
    state_width = state_in.shape[1]
    count = length // BLOCK
    features = layer_input.shape[1]
    spans_of = lax.axis_size("context")
    members = lax.axis_size("tensor")

    layers = [layer_input]
    stride = members // 2
    while stride:
        layers += [swap(layer, "tensor", stride, 2, 1) for layer in layers]
        stride //= 2
    bits = members.bit_length() - 1
    layers = [layers[int(format(hop, f"0{bits}b")[::-1], 2)] for hop in range(members)]

    fetched = [grad_out, state_out, log_decay, state_in, step_size, conv_pre, conv_taps]
    payload, states, grad_here, output_here, decay_here, input_here, step_here, pre_here, taps_here = call(
        functools.partial(state_body, heads, len(fetched) - 3),
        [((state_width + PAD, width), BF16), ((count, state_width + ROW, width), F32)]
        + [(a.shape, a.dtype) for a in fetched],
        fetched,
        hbm=len(fetched),
        scratch=[pltpu.SemaphoreType.DMA((len(fetched),))],
        flops=2 * length * width * state_width,
        moved=2 * length * width,
        vmem=12,
    )

    base, coef = call(
        functools.partial(within_body, heads),
        [((length, width), F32), ((length, width), F32)],
        [skip_gain, input_here, output_here, grad_here, step_here, decay_here, pre_here],
        scalars=1,
        flops=64 * length * width * BLOCK * 8,
        moved=12 * length * width,
        vmem=16,
    )

    stages = radices(spans_of, 4)
    stride, held = 1, []
    for radix in stages:
        last = stride * radix == spans_of
        received = [swap(payload, "context", stride, radix, hop, last) for hop in range(1, radix)]
        if not last:
            following = stages[stages.index(radix) + 1] if len(stages) == 2 else 4
            rows = state_width if following == 2 else state_width + PAD
            payload, *held = call(
                functools.partial(merge_body, radix, stride, not held),
                [((rows, width), BF16), ((state_width + ROW, width), F32)],
                [payload, *received, *held, base],
                idle=1,
            )
            stride *= radix

    *layers, ends = call(
        functools.partial(turn_body, members),
        [((features, length), BF16)] * members + [((members, PAD, features), BF16)],
        layers,
        moved=2 * members * features * length,
    )
    ends = lax.ppermute(ends, "context", [(i, i + 1) for i in range(spans_of - 1)])

    total_rows = members * features
    chunk = total_rows // spans_of
    scaling = 1.0 / math.sqrt(length * spans_of)
    split_shape = (spans_of // 2, chunk, width // 2)
    keep_near, send_near, keep_far, send_far, grads = call(
        functools.partial(tail_body, stages[-1], stride, not held, members, chunk),
        [(split_shape, F32), (split_shape, BF16), (split_shape, F32), (split_shape, BF16), ((PAD + length, width), BF16)],
        [*received, *held, states, base, coef, input_here, taps_here, ends, *layers],
        scratch=[pltpu.VMEM((length + 2 * PAD, width), F32)],
        flops=2 * length * width * total_rows,
        moved=16 * length * width,
        vmem=16,
    )

    got_near = swap(send_near, "context", 1, 2, 1)
    got_far = swap(send_far, "context", 2, 2, 1)

    quarter_shape = (spans_of // 4, chunk, width // 2)
    keep_near, send_near, keep_far, send_far = call(
        halve_both_body,
        [(quarter_shape, F32), (quarter_shape, BF16)] * 2,
        [keep_near, got_near, keep_far, got_far],
        moved=2 * total_rows * width,
        vmem=8,
    )
    got_near = swap(send_near, "context", 2, 2, 1)
    got_far = swap(send_far, "context", 1, 2, 1)
    half = members // 2
    high = PAD + length
    size = -(-half * high // (3 * PAD)) * PAD
    sizes = [min(size, half * high - start) for start in range(0, half * high, size)]
    shares = call(
        functools.partial(share_body, members, sizes),
        [((high, features), F32)] * half + [((size, features), BF16) for size in sizes],
        [grads, value_proj],
        flops=2 * length * width * total_rows,
        moved=8 * length * width,
        vmem=12,
    )
    stride = 1
    share, arrived = shares[:half], [swap(a, "tensor", stride, 2, 1) for a in shares[half:]]
    while half > 1:
        count, half = half, half // 2
        outs = call(
            functools.partial(share_sum_body, count, sizes),
            [((high, features), F32)] * half + [((high, features), BF16)] * half,
            [*share, *arrived],
            moved=4 * length * features,
        )
        stride *= 2
        sizes = [high] * half
        share, arrived = outs[:half], [swap(a, "tensor", stride, 2, 1) for a in outs[half:]]

    joined_shape = (spans_of // 8, chunk, width)
    keep, send = call(
        join_body,
        [(joined_shape, F32), (joined_shape, BF16)],
        [keep_near, got_near, keep_far, got_far],
        moved=total_rows * width,
        vmem=8,
    )
    got, shift = swap(send, "context", 4, 2, 1), 3
    while keep.shape[0] > 1:
        joined_shape = (keep.shape[0] // 2, chunk, width)
        keep, send = call(
            functools.partial(halve_body, shift),
            [(joined_shape, F32), (joined_shape, BF16)],
            [keep, got],
            moved=total_rows * width,
            vmem=8,
        )
        got = swap(send, "context", 1 << shift, 2, 1)
        shift += 1
    head, own = call(
        settle_body,
        [((PAD, features), F32), ((length, features), F32)],
        [*share, *arrived],
    )
    ahead = lax.ppermute(head, "context", [(i + 1, i) for i in range(spans_of - 1)])
    (grad_input,) = call(input_end_body, [((length, features), BF16)], [own, ahead])
    (grad_value_proj,) = call(functools.partial(proj_end_body, scaling), [((chunk, width), F32)], [keep, got])
    return (grad_input, grad_value_proj)


def solution(mesh):
    return jax.shard_map(
        local,
        mesh=mesh,
        in_specs=(
            P("context", "tensor"),
            P(None, "tensor"),
            P(None, "tensor"),
            P("context", "tensor"),
            P("context", None),
            P("context", None),
            P("tensor", "context"),
            P("tensor", "context"),
            P("tensor"),
            P("context", "tensor"),
        ),
        out_specs=(P("context", "tensor"), P("context", "tensor")),
        check_vma=False,
    )
```

```python
import functools
import math

import jax
import jax.numpy as jnp
from jax import lax
from jax.experimental import pallas as pl
from jax.experimental.pallas import tpu as pltpu
from jax.sharding import PartitionSpec as P

CONV = 4
BLOCK = 256
PAD = 16
ROW = 8
F32 = jnp.float32
BF16 = jnp.bfloat16
MIB = 1024 * 1024


def call(body, out_shapes, operands, scalars=0, hbm=0, idle=0, scratch=(), flops=0, moved=0, vmem=8):
    blocks = len(operands) - scalars - hbm - idle
    in_specs = [pl.BlockSpec(memory_space=pltpu.SMEM)] * scalars
    in_specs += [pl.BlockSpec(memory_space=pltpu.VMEM)] * blocks
    in_specs += [pl.BlockSpec(memory_space=pltpu.HBM)] * hbm
    in_specs += [pl.BlockSpec(memory_space=pl.ANY)] * idle
    kept = len(operands) - idle

    def run(*refs):
        body(*refs[:kept], *refs[len(operands) :])

    operands = list(operands)
    for index in range(scalars + blocks, scalars + blocks + hbm):
        operands[index] = pltpu.with_memory_space_constraint(operands[index], pltpu.HBM)
    return pl.pallas_call(
        run,
        out_shape=[jax.ShapeDtypeStruct(shape, kind) for shape, kind in out_shapes],
        in_specs=in_specs,
        out_specs=[pl.BlockSpec(memory_space=pltpu.VMEM)] * len(out_shapes),
        scratch_shapes=list(scratch),
        compiler_params=pltpu.CompilerParams(vmem_limit_bytes=vmem * MIB),
        cost_estimate=pl.CostEstimate(flops=flops, bytes_accessed=moved, transcendentals=0),
    )(*operands)


def radices(count, largest):
    found = []
    while count > 1:
        radix = next(r for r in range(min(largest, count), count + 1) if count % r == 0)
        found.append(radix)
        count //= radix
    return found


def partner(digit, radix, hop):
    if radix & (radix - 1) == 0:
        return digit ^ hop
    return (digit + hop) % radix


def origin(digit, radix, hop):
    if radix & (radix - 1) == 0:
        return digit ^ hop
    return (digit + radix - hop) % radix


def swap(value, axis, stride, radix, hop, back=False):
    count = lax.axis_size(axis)
    pairs = []
    for source in range(count):
        digit = source // stride % radix
        target = source + (partner(digit, radix, hop) - digit) * stride
        if not back or target < source:
            pairs.append((source, target))
    return lax.ppermute(value, axis, pairs)


def dot(a, b, contract):
    return lax.dot_general(a, b, ((contract[:1], contract[1:]), ((), ())), preferred_element_type=F32)


def spread_heads(heads, width):
    lane = lax.broadcasted_iota(jnp.int32, (heads, width), 1)
    head = lax.broadcasted_iota(jnp.int32, (heads, width), 0)
    return (lane // (width // heads) == head).astype(F32)


def spread_scalars(ref, heads, width):
    head = lax.broadcasted_iota(jnp.int32, (1, width), 1) // (width // heads)
    wide = jnp.zeros((1, width), F32)
    for index in range(heads):
        wide = jnp.where(head == index, ref[index], wide)
    return wide


def widen(per_head, spreader):
    high = per_head.astype(BF16).astype(F32)
    parts = jnp.concatenate([high, per_head - high], axis=0).astype(BF16)
    twice = jnp.concatenate([spreader, spreader], axis=0).astype(BF16)
    return dot(parts, twice, (0, 0))


def split(values):
    high = values.astype(BF16).astype(F32)
    middle = (values - high).astype(BF16).astype(F32)
    return high, middle, values - high - middle


def running(decay_blk):
    heads, length = decay_blk.shape
    row = lax.broadcasted_iota(jnp.int32, (length, length), 0)
    column = lax.broadcasted_iota(jnp.int32, (length, length), 1)
    parts = jnp.concatenate(split(decay_blk), axis=0).astype(BF16)
    sums = dot(parts, (row <= column).astype(F32).astype(BF16), (1, 0))
    return sums[:heads] + (sums[heads : 2 * heads] + sums[2 * heads :])


def pack_state(ref, state, decay_row):
    rows = state.shape[0]
    ref[:rows, :] = state.astype(BF16)
    high, middle, low = split(decay_row)
    place = lax.broadcasted_iota(jnp.int32, (PAD, decay_row.shape[1]), 0)
    packed = jnp.where(place == 0, high, jnp.where(place == 1, middle, jnp.where(place == 2, low, 0.0)))
    ref[rows:, :] = packed.astype(BF16)


def unpack_state(ref):
    rows = ref.shape[0] - PAD
    return ref[:rows, :].astype(F32), jnp.sum(ref[rows:, :].astype(F32), axis=0, keepdims=True)


def later_sum(digit, places, states, decays):
    total = None
    span = jnp.zeros_like(decays[0])
    for index, place in enumerate(places):
        between = jnp.zeros_like(decays[0])
        for other, other_place in enumerate(places):
            if other != index:
                inside = jnp.logical_and(other_place > digit, other_place < place)
                between = between + jnp.where(inside, decays[other], 0.0)
        weight = jnp.where(place > digit, jnp.exp(between), 0.0)
        total = weight * states[index] if total is None else total + weight * states[index]
        span = span + jnp.where(place > digit, decays[index], 0.0)
    return total, span


def state_body(heads, others, grad_hbm, output_hbm, decay_hbm, *refs):
    rest, refs = refs[:others], refs[others:]
    payload_ref, states_ref, grad_ref, output_ref, decay_ref = refs[:5]
    rest_out, sems = refs[5:-1], refs[-1]
    pairs = [(grad_hbm, grad_ref), (output_hbm, output_ref), (decay_hbm, decay_ref), *zip(rest, rest_out)]
    copies = [pltpu.make_async_copy(a, b, sems.at[index]) for index, (a, b) in enumerate(pairs)]
    firsts, later = copies[:3], copies[3:]
    for copy in firsts + later:
        copy.start()
    for copy in firsts:
        copy.wait()
    width = grad_ref.shape[1]
    count = grad_ref.shape[0] // BLOCK
    spreader = spread_heads(heads, width)
    states, spans = [], []
    for k in range(count):
        rows = slice(k * BLOCK, (k + 1) * BLOCK)
        cumulative = running(decay_ref[:, rows])
        spans.append(jnp.sum(spreader * cumulative[:, BLOCK - 1 :], axis=0, keepdims=True))
        weighted = (grad_ref[rows, :].astype(F32) * widen(jnp.exp(cumulative), spreader)).astype(BF16)
        states.append(dot(output_ref[rows, :], weighted, (0, 0)))
    total, span = states[-1], spans[-1]
    for k in reversed(range(count - 1)):
        total = states[k] + jnp.exp(spans[k]) * total
        span = span + spans[k]
    pack_state(payload_ref, total, span)
    for k in range(count):
        keep_state(states_ref.at[k], states[k], spans[k])
    for copy in later:
        copy.wait()


def keep_state(ref, state, span):
    rows = state.shape[0]
    ref[:rows, :] = state
    ref[rows:, :] = jnp.broadcast_to(span, (ROW, span.shape[1]))


def kept_state(ref):
    rows = ref.shape[0] - ROW
    return ref[:rows, :], ref[rows : rows + 1, :]


def merge_body(radix, stride, first, payload_ref, *refs):
    received = refs[: radix - 1]
    next_ref, held_out = refs[-2:]
    digit = lax.axis_index("context") // stride % radix
    pairs = [unpack_state(ref) for ref in (payload_ref, *received)]
    states, decays = [a for a, _ in pairs], [b for _, b in pairs]
    places = [origin(digit, radix, hop) for hop in range(radix)]
    whole, whole_span = later_sum(-1, places, states, decays)
    if next_ref.shape[0] > whole.shape[0]:
        pack_state(next_ref, whole, whole_span)
    else:
        next_ref[...] = whole.astype(BF16)
    later, span = later_sum(digit, places[1:], states[1:], decays[1:])
    if not first:
        held, reach = kept_state(refs[radix - 1])
        later = held + jnp.exp(reach) * later
        span = reach + span
    keep_state(held_out, later, span)


def within_body(heads, skip_ref, *refs):
    input_ref, output_ref, grad_ref, step_ref, decay_ref, pre_ref, base_ref, coef_ref = refs
    for k in range(grad_ref.shape[0] // BLOCK):
        rows = slice(k * BLOCK, (k + 1) * BLOCK)
        within_block(
            heads,
            skip_ref,
            *(ref.at[rows, :] for ref in (input_ref, output_ref, grad_ref)),
            *(ref.at[:, rows] for ref in (step_ref, decay_ref)),
            *(ref.at[rows, :] for ref in (pre_ref, base_ref, coef_ref)),
        )


def within_block(heads, skip_ref, input_ref, output_ref, grad_ref, step_ref, decay_ref, pre_ref, base_ref, coef_ref):
    width = grad_ref.shape[1]
    head_width = width // heads
    group = max(1, 128 // head_width)
    half = BLOCK // 2
    spreader = spread_heads(heads, width)
    cumulative = running(decay_ref[...])
    across = cumulative.T
    scores = dot(input_ref[...], output_ref[...], (1, 1))
    step = step_ref[...]
    step_wide = widen(step, spreader)
    reach_wide = widen(step * jnp.exp(cumulative[:, BLOCK - 1 :] - cumulative), spreader)
    skip_wide = spread_scalars(skip_ref, heads, width)
    row = lax.broadcasted_iota(jnp.int32, (half, half), 0)
    column = lax.broadcasted_iota(jnp.int32, (half, half), 1)
    keep = column >= row
    lane = lax.broadcasted_iota(jnp.int32, (half, group * head_width), 1) // head_width

    def weigh(head, rows, columns, diagonal):
        spread = cumulative[head : head + 1, columns] - across[rows, head : head + 1]
        if diagonal:
            spread = jnp.where(keep, spread, -jnp.inf)
        return (scores[rows, columns] * jnp.exp(spread)).astype(BF16)

    first, second = slice(0, half), slice(half, BLOCK)
    for start in range(0, heads, group):
        channels = slice(start * head_width, (start + group) * head_width)
        grads = grad_ref[:, channels]
        upper = lower = None
        for member in range(group):
            head = start + member
            top = jnp.concatenate([weigh(head, first, first, True), weigh(head, first, second, False)], axis=1)
            one = dot(top, grads, (1, 0))
            two = dot(weigh(head, second, second, True), grads[half:, :], (1, 0))
            upper = one if upper is None else jnp.where(lane == member, one, upper)
            lower = two if lower is None else jnp.where(lane == member, two, lower)
        for rows, product in ((first, upper), (second, lower)):
            pre = pre_ref[rows, channels].astype(F32)
            gate = 1.0 / (1.0 + jnp.exp(-pre))
            slope = gate * (1.0 + pre * (1.0 - gate))
            direct = step_wide[rows, channels] * product + skip_wide[:, channels] * grads[rows, :].astype(F32)
            base_ref[rows, channels] = slope * direct
            coef_ref[rows, channels] = slope * reach_wide[rows, channels]


def turn_body(members, *refs):
    pieces, turned_ref, ends_ref = refs[:members], refs[members], refs[-1]
    length, features = pieces[0].shape
    for hop in range(members):
        source = origin(lax.axis_index("tensor"), members, hop)
        ends_ref[source] = pieces[hop][length - PAD :, :]
        start = pl.multiple_of(source * features, features)
        turned_ref[pl.ds(start, features), :] = pieces[hop][...].T


def tail_body(radix, stride, first, members, chunk, *refs):
    received, refs = refs[: radix - 1], refs[radix - 1 :]
    if not first:
        held_ref, refs = refs[0], refs[1:]
    states_ref, base_ref, coef_ref, input_ref, taps_ref, ends_ref, layer_ref = refs[:7]
    send_near, send_far, grads_ref, turned_ref, conv_ref = refs[7:]
    length, width = base_ref.shape
    place = lax.axis_index("context")
    digit = place // stride % radix
    if radix == 2:
        carry = jnp.where(digit == 0, received[0][...].astype(F32), 0.0)
    else:
        pairs = [unpack_state(ref) for ref in received]
        places = [origin(digit, radix, hop) for hop in range(1, radix)]
        carry, _ = later_sum(digit, places, [a for a, _ in pairs], [b for _, b in pairs])
    if not first:
        held, reach = kept_state(held_ref)
        carry = held + jnp.exp(reach) * carry
    conv_ref[:PAD, :] = jnp.zeros((PAD, width), F32)
    conv_ref[PAD + length :, :] = jnp.zeros((PAD, width), F32)
    for k in reversed(range(length // BLOCK)):
        rows = slice(k * BLOCK, (k + 1) * BLOCK)
        product = dot(input_ref[rows, :], carry.astype(BF16), (1, 0))
        value = base_ref[rows, :] + coef_ref[rows, :] * product
        conv_ref[PAD + k * BLOCK : PAD + (k + 1) * BLOCK, :] = value.astype(BF16).astype(F32)
        if k:
            state, span = kept_state(states_ref.at[k])
            carry = state + jnp.exp(span) * carry
    total = None
    for offset in range(CONV):
        shift = CONV - 1 - offset
        term = taps_ref[offset : offset + 1, :] * conv_ref[shift : shift + PAD + length, :]
        total = term if total is None else total + term
    grads_ref[...] = total.astype(BF16)
    features = ends_ref.shape[2]
    for index in range(members):
        turned_ref[index * features : (index + 1) * features, :] = ends_ref[index].T
    products(chunk, 1, layer_ref, turned_ref, grads_ref, send_near, send_far)


def products(chunk, flip, layer_ref, turned_ref, grads_ref, near_ref, far_ref):
    place = lax.axis_index("context")
    near_bit, far_bit = (place & 1) ^ flip, ((place >> 1) & 1) ^ flip
    half = near_ref.shape[2]
    for channels, out_ref, number in (
        (slice(0, half), near_ref, lambda i: 2 * i + near_bit),
        (slice(half, 2 * half), far_ref, lambda i: (i & 1) + ((i >> 1) << 2) + 2 * far_bit),
    ):
        starts = [pl.multiple_of(number(i) * chunk, chunk) for i in range(out_ref.shape[0])]
        layers = jnp.concatenate([layer_ref[pl.ds(start, chunk), :] for start in starts], axis=0)
        ends = jnp.concatenate([turned_ref[pl.ds(start, chunk), :] for start in starts], axis=0)
        product = dot(layers, grads_ref[PAD:, channels], (1, 0)) + dot(ends, grads_ref[:PAD, channels], (1, 0))
        for i in range(out_ref.shape[0]):
            out_ref[i] = product[i * chunk : (i + 1) * chunk, :].astype(out_ref.dtype)


def kept_body(chunk, layer_ref, turned_ref, grads_ref, keep_near, keep_far):
    products(chunk, 0, layer_ref, turned_ref, grads_ref, keep_near, keep_far)


def overlaps(index, high, sizes):
    start, found = 0, []
    for part, size in enumerate(sizes):
        first, last = max(start, index * high), min(start + size, (index + 1) * high)
        if first < last:
            found.append((part, slice(first - start, last - start), slice(first - index * high, last - index * high)))
        start += size
    return found


def share_body(members, sizes, grads_ref, proj_ref, *refs):
    keep_refs, send_refs = refs[: members // 2], refs[members // 2 :]
    high, features = keep_refs[0].shape
    for hop in range(members):
        goal = lax.axis_index("tensor") ^ hop
        block = proj_ref[pl.ds(pl.multiple_of(goal * features, features), features), :]
        share = dot(grads_ref[...], block, (1, 1))
        if hop % 2:
            for part, there, here in overlaps(hop // 2, high, sizes):
                send_refs[part][there, :] = share[here, :].astype(BF16)
        else:
            keep_refs[hop // 2][...] = share


def share_sum_body(count, sizes, *refs):
    keeps, arrivals, outs = refs[:count], refs[count : count + len(sizes)], refs[count + len(sizes) :]
    for index in range(count):
        out = outs[index // 2 + index % 2 * (count // 2)]
        for part, there, here in overlaps(index, out.shape[0], sizes):
            out[here, :] = (keeps[index][here, :] + arrivals[part][there, :].astype(F32)).astype(out.dtype)


def settle_body(share_ref, arrived_ref, head_ref, own_ref):
    head_ref[...] = share_ref[:PAD, :] + arrived_ref[:PAD, :].astype(F32)
    own_ref[...] = share_ref[PAD:, :] + arrived_ref[PAD:, :].astype(F32)


def end_body(scaling, keep_ref, got_ref, own_ref, ahead_ref, proj_out, input_out):
    proj_out[...] = (keep_ref[0] + got_ref[0].astype(F32)) * scaling
    rest = own_ref.shape[0] - PAD
    input_out[:rest, :] = own_ref[:rest, :].astype(BF16)
    input_out[rest:, :] = (own_ref[rest:, :] + ahead_ref[...]).astype(BF16)


def halve(bit, keep_ref, received_ref, keep_out, send_out):
    for index in range(keep_out.shape[0]):
        mine, other = 2 * index + bit, 2 * index + 1 - bit
        keep_out[index] = keep_ref[mine] + received_ref[mine].astype(F32)
        send_out[index] = (keep_ref[other] + received_ref[other].astype(F32)).astype(BF16)


def bit_of_place(shift):
    return (lax.axis_index("context") >> shift) & 1


def halve_body(shift, keep_ref, received_ref, keep_out, send_out):
    halve(bit_of_place(shift), keep_ref, received_ref, keep_out, send_out)


def halve_both_body(keep_near, got_near, keep_far, got_far, near_out, near_send, far_out, far_send):
    halve(bit_of_place(1), keep_near, got_near, near_out, near_send)
    halve(bit_of_place(0), keep_far, got_far, far_out, far_send)


def join_body(keep_near, got_near, keep_far, got_far, keep_out, send_out):
    bit = bit_of_place(2)
    half = keep_near.shape[2]
    halve(bit, keep_near, got_near, keep_out.at[:, :, :half], send_out.at[:, :, :half])
    halve(bit, keep_far, got_far, keep_out.at[:, :, half:], send_out.at[:, :, half:])


def local(
    layer_input,
    value_proj,
    conv_taps,
    conv_pre,
    state_in,
    state_out,
    step_size,
    log_decay,
    skip_gain,
    grad_out,
):
    length, width = grad_out.shape
    heads = step_size.shape[0]
    state_width = state_in.shape[1]
    count = length // BLOCK
    features = layer_input.shape[1]
    spans_of = lax.axis_size("context")
    members = lax.axis_size("tensor")

    layers = [layer_input]
    stride = members // 2
    while stride:
        layers += [swap(layer, "tensor", stride, 2, 1) for layer in layers]
        stride //= 2
    bits = members.bit_length() - 1
    layers = [layers[int(format(hop, f"0{bits}b")[::-1], 2)] for hop in range(members)]

    fetched = [grad_out, state_out, log_decay, state_in, step_size, conv_pre, conv_taps]
    payload, states, grad_here, output_here, decay_here, input_here, step_here, pre_here, taps_here = call(
        functools.partial(state_body, heads, len(fetched) - 3),
        [((state_width + PAD, width), BF16), ((count, state_width + ROW, width), F32)]
        + [(a.shape, a.dtype) for a in fetched],
        fetched,
        hbm=len(fetched),
        scratch=[pltpu.SemaphoreType.DMA((len(fetched),))],
        flops=2 * length * width * state_width,
        moved=2 * length * width,
        vmem=12,
    )

    base, coef = call(
        functools.partial(within_body, heads),
        [((length, width), F32), ((length, width), F32)],
        [skip_gain, input_here, output_here, grad_here, step_here, decay_here, pre_here],
        scalars=1,
        flops=64 * length * width * BLOCK * 8,
        moved=12 * length * width,
        vmem=16,
    )

    stages = radices(spans_of, 4)
    stride, held = 1, []
    for radix in stages:
        last = stride * radix == spans_of
        received = [swap(payload, "context", stride, radix, hop, last) for hop in range(1, radix)]
        if not last:
            following = stages[stages.index(radix) + 1] if len(stages) == 2 else 4
            rows = state_width if following == 2 else state_width + PAD
            payload, *held = call(
                functools.partial(merge_body, radix, stride, not held),
                [((rows, width), BF16), ((state_width + ROW, width), F32)],
                [payload, *received, *held, base],
                idle=1,
            )
            stride *= radix

    turned, ends = call(
        functools.partial(turn_body, members),
        [((members * features, length), BF16), ((members, PAD, features), BF16)],
        layers,
        moved=2 * members * features * length,
    )
    ends = lax.ppermute(ends, "context", [(i, i + 1) for i in range(spans_of - 1)])

    total_rows = members * features
    chunk = total_rows // spans_of
    scaling = 1.0 / math.sqrt(length * spans_of)
    split_shape = (spans_of // 2, chunk, width // 2)
    send_near, send_far, grads, turned_ends = call(
        functools.partial(tail_body, stages[-1], stride, not held, members, chunk),
        [(split_shape, BF16), (split_shape, BF16), ((PAD + length, width), BF16), ((total_rows, PAD), BF16)],
        [*received, *held, states, base, coef, input_here, taps_here, ends, turned],
        scratch=[pltpu.VMEM((length + 2 * PAD, width), F32)],
        flops=2 * length * width * total_rows,
        moved=16 * length * width,
        vmem=16,
    )
    keep_near, keep_far = call(
        functools.partial(kept_body, chunk),
        [(split_shape, F32), (split_shape, F32)],
        [turned, turned_ends, grads],
        flops=length * width * total_rows,
        moved=8 * length * width,
    )

    got_near = swap(send_near, "context", 1, 2, 1)
    got_far = swap(send_far, "context", 2, 2, 1)

    quarter_shape = (spans_of // 4, chunk, width // 2)
    keep_near, send_near, keep_far, send_far = call(
        halve_both_body,
        [(quarter_shape, F32), (quarter_shape, BF16)] * 2,
        [keep_near, got_near, keep_far, got_far],
        moved=2 * total_rows * width,
        vmem=8,
    )
    got_near = swap(send_near, "context", 2, 2, 1)
    got_far = swap(send_far, "context", 1, 2, 1)
    half = members // 2
    high = PAD + length
    size = -(-half * high // (3 * PAD)) * PAD
    sizes = [min(size, half * high - start) for start in range(0, half * high, size)]
    shares = call(
        functools.partial(share_body, members, sizes),
        [((high, features), F32)] * half + [((size, features), BF16) for size in sizes],
        [grads, value_proj],
        flops=2 * length * width * total_rows,
        moved=8 * length * width,
        vmem=12,
    )
    stride = 1
    share, arrived = shares[:half], [swap(a, "tensor", stride, 2, 1) for a in shares[half:]]
    while half > 1:
        count, half = half, half // 2
        outs = call(
            functools.partial(share_sum_body, count, sizes),
            [((high, features), F32)] * half + [((high, features), BF16)] * half,
            [*share, *arrived],
            moved=4 * length * features,
        )
        stride *= 2
        sizes = [high] * half
        share, arrived = outs[:half], [swap(a, "tensor", stride, 2, 1) for a in outs[half:]]

    joined_shape = (spans_of // 8, chunk, width)
    keep, send = call(
        join_body,
        [(joined_shape, F32), (joined_shape, BF16)],
        [keep_near, got_near, keep_far, got_far],
        moved=total_rows * width,
        vmem=8,
    )
    got, shift = swap(send, "context", 4, 2, 1), 3
    while keep.shape[0] > 1:
        joined_shape = (keep.shape[0] // 2, chunk, width)
        keep, send = call(
            functools.partial(halve_body, shift),
            [(joined_shape, F32), (joined_shape, BF16)],
            [keep, got],
            moved=total_rows * width,
            vmem=8,
        )
        got = swap(send, "context", 1 << shift, 2, 1)
        shift += 1
    head, own = call(
        settle_body,
        [((PAD, features), F32), ((length, features), F32)],
        [*share, *arrived],
    )
    ahead = lax.ppermute(head, "context", [(i + 1, i) for i in range(spans_of - 1)])
    grad_value_proj, grad_input = call(
        functools.partial(end_body, scaling),
        [((chunk, width), F32), ((length, features), BF16)],
        [keep, got, own, ahead],
    )
    return (grad_input, grad_value_proj)


def solution(mesh):
    return jax.shard_map(
        local,
        mesh=mesh,
        in_specs=(
            P("context", "tensor"),
            P(None, "tensor"),
            P(None, "tensor"),
            P("context", "tensor"),
            P("context", None),
            P("context", None),
            P("tensor", "context"),
            P("tensor", "context"),
            P("tensor"),
            P("context", "tensor"),
        ),
        out_specs=(P("context", "tensor"), P("context", "tensor")),
        check_vma=False,
    )
```

```python
import functools
import math

import jax
import jax.numpy as jnp
from jax import lax
from jax.experimental import pallas as pl
from jax.experimental.pallas import tpu as pltpu
from jax.sharding import PartitionSpec as P

CONV = 4
BLOCK = 256
PAD = 16
ROW = 8
F32 = jnp.float32
BF16 = jnp.bfloat16
MIB = 1024 * 1024


def call(body, out_shapes, operands, scalars=0, hbm=0, idle=0, scratch=(), flops=0, moved=0, vmem=8):
    blocks = len(operands) - scalars - hbm - idle
    in_specs = [pl.BlockSpec(memory_space=pltpu.SMEM)] * scalars
    in_specs += [pl.BlockSpec(memory_space=pltpu.VMEM)] * blocks
    in_specs += [pl.BlockSpec(memory_space=pltpu.HBM)] * hbm
    in_specs += [pl.BlockSpec(memory_space=pl.ANY)] * idle
    kept = len(operands) - idle

    def run(*refs):
        body(*refs[:kept], *refs[len(operands) :])

    operands = list(operands)
    for index in range(scalars + blocks, scalars + blocks + hbm):
        operands[index] = pltpu.with_memory_space_constraint(operands[index], pltpu.HBM)
    return pl.pallas_call(
        run,
        out_shape=[jax.ShapeDtypeStruct(shape, kind) for shape, kind in out_shapes],
        in_specs=in_specs,
        out_specs=[pl.BlockSpec(memory_space=pltpu.VMEM)] * len(out_shapes),
        scratch_shapes=list(scratch),
        compiler_params=pltpu.CompilerParams(vmem_limit_bytes=vmem * MIB),
        cost_estimate=pl.CostEstimate(flops=flops, bytes_accessed=moved, transcendentals=0),
    )(*operands)


def radices(count, largest):
    found = []
    while count > 1:
        radix = next(r for r in range(min(largest, count), count + 1) if count % r == 0)
        found.append(radix)
        count //= radix
    return found


def partner(digit, radix, hop):
    if radix & (radix - 1) == 0:
        return digit ^ hop
    return (digit + hop) % radix


def origin(digit, radix, hop):
    if radix & (radix - 1) == 0:
        return digit ^ hop
    return (digit + radix - hop) % radix


def swap(value, axis, stride, radix, hop, back=False):
    count = lax.axis_size(axis)
    pairs = []
    for source in range(count):
        digit = source // stride % radix
        target = source + (partner(digit, radix, hop) - digit) * stride
        if not back or target < source:
            pairs.append((source, target))
    return lax.ppermute(value, axis, pairs)


def dot(a, b, contract):
    return lax.dot_general(a, b, ((contract[:1], contract[1:]), ((), ())), preferred_element_type=F32)


def spread_heads(heads, width):
    lane = lax.broadcasted_iota(jnp.int32, (heads, width), 1)
    head = lax.broadcasted_iota(jnp.int32, (heads, width), 0)
    return (lane // (width // heads) == head).astype(F32)


def spread_scalars(ref, heads, width):
    head = lax.broadcasted_iota(jnp.int32, (1, width), 1) // (width // heads)
    wide = jnp.zeros((1, width), F32)
    for index in range(heads):
        wide = jnp.where(head == index, ref[index], wide)
    return wide


def widen(per_head, spreader):
    high = per_head.astype(BF16).astype(F32)
    parts = jnp.concatenate([high, per_head - high], axis=0).astype(BF16)
    twice = jnp.concatenate([spreader, spreader], axis=0).astype(BF16)
    return dot(parts, twice, (0, 0))


def split(values):
    high = values.astype(BF16).astype(F32)
    middle = (values - high).astype(BF16).astype(F32)
    return high, middle, values - high - middle


def running(decay_blk):
    heads, length = decay_blk.shape
    row = lax.broadcasted_iota(jnp.int32, (length, length), 0)
    column = lax.broadcasted_iota(jnp.int32, (length, length), 1)
    parts = jnp.concatenate(split(decay_blk), axis=0).astype(BF16)
    sums = dot(parts, (row <= column).astype(F32).astype(BF16), (1, 0))
    return sums[:heads] + (sums[heads : 2 * heads] + sums[2 * heads :])


def pack_state(ref, state, decay_row):
    rows = state.shape[0]
    ref[:rows, :] = state.astype(BF16)
    high, middle, low = split(decay_row)
    place = lax.broadcasted_iota(jnp.int32, (PAD, decay_row.shape[1]), 0)
    packed = jnp.where(place == 0, high, jnp.where(place == 1, middle, jnp.where(place == 2, low, 0.0)))
    ref[rows:, :] = packed.astype(BF16)


def unpack_state(ref):
    rows = ref.shape[0] - PAD
    return ref[:rows, :].astype(F32), jnp.sum(ref[rows:, :].astype(F32), axis=0, keepdims=True)


def later_sum(digit, places, states, decays):
    total = None
    span = jnp.zeros_like(decays[0])
    for index, place in enumerate(places):
        between = jnp.zeros_like(decays[0])
        for other, other_place in enumerate(places):
            if other != index:
                inside = jnp.logical_and(other_place > digit, other_place < place)
                between = between + jnp.where(inside, decays[other], 0.0)
        weight = jnp.where(place > digit, jnp.exp(between), 0.0)
        total = weight * states[index] if total is None else total + weight * states[index]
        span = span + jnp.where(place > digit, decays[index], 0.0)
    return total, span


def state_body(heads, others, grad_hbm, output_hbm, decay_hbm, *refs):
    rest, refs = refs[:others], refs[others:]
    payload_ref, states_ref, grad_ref, output_ref, decay_ref = refs[:5]
    rest_out, sems = refs[5:-1], refs[-1]
    pairs = [(grad_hbm, grad_ref), (output_hbm, output_ref), (decay_hbm, decay_ref), *zip(rest, rest_out)]
    copies = [pltpu.make_async_copy(a, b, sems.at[index]) for index, (a, b) in enumerate(pairs)]
    firsts, later = copies[:3], copies[3:]
    for copy in firsts + later:
        copy.start()
    for copy in firsts:
        copy.wait()
    width = grad_ref.shape[1]
    count = grad_ref.shape[0] // BLOCK
    spreader = spread_heads(heads, width)
    states, spans = [], []
    for k in range(count):
        rows = slice(k * BLOCK, (k + 1) * BLOCK)
        cumulative = running(decay_ref[:, rows])
        spans.append(jnp.sum(spreader * cumulative[:, BLOCK - 1 :], axis=0, keepdims=True))
        weighted = (grad_ref[rows, :].astype(F32) * widen(jnp.exp(cumulative), spreader)).astype(BF16)
        states.append(dot(output_ref[rows, :], weighted, (0, 0)))
    total, span = states[-1], spans[-1]
    for k in reversed(range(count - 1)):
        total = states[k] + jnp.exp(spans[k]) * total
        span = span + spans[k]
    pack_state(payload_ref, total, span)
    for k in range(count):
        keep_state(states_ref.at[k], states[k], spans[k])
    for copy in later:
        copy.wait()


def keep_state(ref, state, span):
    rows = state.shape[0]
    ref[:rows, :] = state
    ref[rows:, :] = jnp.broadcast_to(span, (ROW, span.shape[1]))


def kept_state(ref):
    rows = ref.shape[0] - ROW
    return ref[:rows, :], ref[rows : rows + 1, :]


def merge_body(radix, stride, first, payload_ref, *refs):
    received = refs[: radix - 1]
    next_ref, held_out = refs[-2:]
    digit = lax.axis_index("context") // stride % radix
    pairs = [unpack_state(ref) for ref in (payload_ref, *received)]
    states, decays = [a for a, _ in pairs], [b for _, b in pairs]
    places = [origin(digit, radix, hop) for hop in range(radix)]
    whole, whole_span = later_sum(-1, places, states, decays)
    if next_ref.shape[0] > whole.shape[0]:
        pack_state(next_ref, whole, whole_span)
    else:
        next_ref[...] = whole.astype(BF16)
    later, span = later_sum(digit, places[1:], states[1:], decays[1:])
    if not first:
        held, reach = kept_state(refs[radix - 1])
        later = held + jnp.exp(reach) * later
        span = reach + span
    keep_state(held_out, later, span)


def within_body(heads, skip_ref, *refs):
    input_ref, output_ref, grad_ref, step_ref, decay_ref, pre_ref, base_ref, coef_ref = refs
    for k in range(grad_ref.shape[0] // BLOCK):
        rows = slice(k * BLOCK, (k + 1) * BLOCK)
        within_block(
            heads,
            skip_ref,
            *(ref.at[rows, :] for ref in (input_ref, output_ref, grad_ref)),
            *(ref.at[:, rows] for ref in (step_ref, decay_ref)),
            *(ref.at[rows, :] for ref in (pre_ref, base_ref, coef_ref)),
        )


def within_block(heads, skip_ref, input_ref, output_ref, grad_ref, step_ref, decay_ref, pre_ref, base_ref, coef_ref):
    width = grad_ref.shape[1]
    head_width = width // heads
    group = max(1, 128 // head_width)
    half = BLOCK // 2
    spreader = spread_heads(heads, width)
    cumulative = running(decay_ref[...])
    across = cumulative.T
    scores = dot(input_ref[...], output_ref[...], (1, 1))
    step = step_ref[...]
    step_wide = widen(step, spreader)
    reach_wide = widen(step * jnp.exp(cumulative[:, BLOCK - 1 :] - cumulative), spreader)
    skip_wide = spread_scalars(skip_ref, heads, width)
    row = lax.broadcasted_iota(jnp.int32, (half, half), 0)
    column = lax.broadcasted_iota(jnp.int32, (half, half), 1)
    keep = column >= row
    lane = lax.broadcasted_iota(jnp.int32, (half, group * head_width), 1) // head_width

    def weigh(head, rows, columns, diagonal):
        spread = cumulative[head : head + 1, columns] - across[rows, head : head + 1]
        if diagonal:
            spread = jnp.where(keep, spread, -jnp.inf)
        return (scores[rows, columns] * jnp.exp(spread)).astype(BF16)

    first, second = slice(0, half), slice(half, BLOCK)
    for start in range(0, heads, group):
        channels = slice(start * head_width, (start + group) * head_width)
        grads = grad_ref[:, channels]
        upper = lower = None
        for member in range(group):
            head = start + member
            top = jnp.concatenate([weigh(head, first, first, True), weigh(head, first, second, False)], axis=1)
            one = dot(top, grads, (1, 0))
            two = dot(weigh(head, second, second, True), grads[half:, :], (1, 0))
            upper = one if upper is None else jnp.where(lane == member, one, upper)
            lower = two if lower is None else jnp.where(lane == member, two, lower)
        for rows, product in ((first, upper), (second, lower)):
            pre = pre_ref[rows, channels].astype(F32)
            gate = 1.0 / (1.0 + jnp.exp(-pre))
            slope = gate * (1.0 + pre * (1.0 - gate))
            direct = step_wide[rows, channels] * product + skip_wide[:, channels] * grads[rows, :].astype(F32)
            base_ref[rows, channels] = slope * direct
            coef_ref[rows, channels] = slope * reach_wide[rows, channels]


def turn_body(members, *refs):
    pieces, turned_ref, ends_ref = refs[:members], refs[members], refs[-1]
    length, features = pieces[0].shape
    for hop in range(members):
        source = origin(lax.axis_index("tensor"), members, hop)
        ends_ref[source] = pieces[hop][length - PAD :, :]
        start = pl.multiple_of(source * features, features)
        turned_ref[pl.ds(start, features), :] = pieces[hop][...].T


def tail_body(radix, stride, first, members, chunk, *refs):
    received, refs = refs[: radix - 1], refs[radix - 1 :]
    if not first:
        held_ref, refs = refs[0], refs[1:]
    states_ref, base_ref, coef_ref, input_ref, taps_ref, ends_ref, layer_ref = refs[:7]
    send_near, send_far, grads_ref, turned_ref, conv_ref = refs[7:]
    length, width = base_ref.shape
    place = lax.axis_index("context")
    digit = place // stride % radix
    if radix == 2:
        carry = jnp.where(digit == 0, received[0][...].astype(F32), 0.0)
    else:
        pairs = [unpack_state(ref) for ref in received]
        places = [origin(digit, radix, hop) for hop in range(1, radix)]
        carry, _ = later_sum(digit, places, [a for a, _ in pairs], [b for _, b in pairs])
    if not first:
        held, reach = kept_state(held_ref)
        carry = held + jnp.exp(reach) * carry
    conv_ref[:PAD, :] = jnp.zeros((PAD, width), F32)
    conv_ref[PAD + length :, :] = jnp.zeros((PAD, width), F32)
    for k in reversed(range(length // BLOCK)):
        rows = slice(k * BLOCK, (k + 1) * BLOCK)
        product = dot(input_ref[rows, :], carry.astype(BF16), (1, 0))
        value = base_ref[rows, :] + coef_ref[rows, :] * product
        conv_ref[PAD + k * BLOCK : PAD + (k + 1) * BLOCK, :] = value.astype(BF16).astype(F32)
        if k:
            state, span = kept_state(states_ref.at[k])
            carry = state + jnp.exp(span) * carry
    total = None
    for offset in range(CONV):
        shift = CONV - 1 - offset
        term = taps_ref[offset : offset + 1, :] * conv_ref[shift : shift + PAD + length, :]
        total = term if total is None else total + term
    grads_ref[...] = total.astype(BF16)
    features = ends_ref.shape[2]
    for index in range(members):
        turned_ref[index * features : (index + 1) * features, :] = ends_ref[index].T
    products(chunk, 1, layer_ref, turned_ref, grads_ref, send_near, send_far)


def products(chunk, flip, layer_ref, turned_ref, grads_ref, near_ref, far_ref):
    place = lax.axis_index("context")
    near_bit, far_bit = (place & 1) ^ flip, ((place >> 1) & 1) ^ flip
    half = near_ref.shape[2]
    for channels, out_ref, number in (
        (slice(0, half), near_ref, lambda i: 2 * i + near_bit),
        (slice(half, 2 * half), far_ref, lambda i: (i & 1) + ((i >> 1) << 2) + 2 * far_bit),
    ):
        starts = [pl.multiple_of(number(i) * chunk, chunk) for i in range(out_ref.shape[0])]
        layers = jnp.concatenate([layer_ref[pl.ds(start, chunk), :] for start in starts], axis=0)
        ends = jnp.concatenate([turned_ref[pl.ds(start, chunk), :] for start in starts], axis=0)
        product = dot(layers, grads_ref[PAD:, channels], (1, 0)) + dot(ends, grads_ref[:PAD, channels], (1, 0))
        for i in range(out_ref.shape[0]):
            out_ref[i] = product[i * chunk : (i + 1) * chunk, :].astype(out_ref.dtype)


def kept_body(chunk, layer_ref, turned_ref, grads_ref, keep_near, keep_far):
    products(chunk, 0, layer_ref, turned_ref, grads_ref, keep_near, keep_far)


def overlaps(index, high, sizes):
    start, found = 0, []
    for part, size in enumerate(sizes):
        first, last = max(start, index * high), min(start + size, (index + 1) * high)
        if first < last:
            found.append((part, slice(first - start, last - start), slice(first - index * high, last - index * high)))
        start += size
    return found


def share_body(members, sizes, grads_ref, proj_ref, *refs):
    keep_refs, send_refs = refs[: members // 2], refs[members // 2 :]
    high, features = keep_refs[0].shape
    for hop in range(members):
        goal = lax.axis_index("tensor") ^ hop
        block = proj_ref[pl.ds(pl.multiple_of(goal * features, features), features), :]
        share = dot(grads_ref[...], block, (1, 1))
        if hop % 2:
            for part, there, here in overlaps(hop // 2, high, sizes):
                send_refs[part][there, :] = share[here, :].astype(BF16)
        else:
            keep_refs[hop // 2][...] = share


def share_sum_body(count, sizes, *refs):
    keeps, arrivals, outs = refs[:count], refs[count : count + len(sizes)], refs[count + len(sizes) :]
    for index in range(count):
        out = outs[index // 2 + index % 2 * (count // 2)]
        for part, there, here in overlaps(index, out.shape[0], sizes):
            out[here, :] = (keeps[index][here, :] + arrivals[part][there, :].astype(F32)).astype(out.dtype)


def settle_body(share_ref, arrived_ref, head_ref, own_ref):
    head_ref[...] = share_ref[:PAD, :] + arrived_ref[:PAD, :].astype(F32)
    own_ref[...] = share_ref[PAD:, :] + arrived_ref[PAD:, :].astype(F32)


def end_body(scaling, keep_ref, got_ref, own_ref, ahead_ref, proj_out, input_out):
    proj_out[...] = (keep_ref[0] + got_ref[0].astype(F32)) * scaling
    rest = own_ref.shape[0] - PAD
    input_out[:rest, :] = own_ref[:rest, :].astype(BF16)
    input_out[rest:, :] = (own_ref[rest:, :] + ahead_ref[...]).astype(BF16)


def halve(bit, keep_ref, received_ref, keep_out, send_out):
    for index in range(keep_out.shape[0]):
        mine, other = 2 * index + bit, 2 * index + 1 - bit
        keep_out[index] = keep_ref[mine] + received_ref[mine].astype(F32)
        send_out[index] = (keep_ref[other] + received_ref[other].astype(F32)).astype(BF16)


def bit_of_place(shift):
    return (lax.axis_index("context") >> shift) & 1


def halve_body(shift, keep_ref, received_ref, keep_out, send_out):
    halve(bit_of_place(shift), keep_ref, received_ref, keep_out, send_out)


def halve_both_body(keep_near, got_near, keep_far, got_far, near_out, near_send, far_out, far_send):
    halve(bit_of_place(1), keep_near, got_near, near_out, near_send)
    halve(bit_of_place(0), keep_far, got_far, far_out, far_send)


def join_body(keep_near, got_near, keep_far, got_far, keep_out, send_out):
    bit = bit_of_place(2)
    half = keep_near.shape[2]
    halve(bit, keep_near, got_near, keep_out.at[:, :, :half], send_out.at[:, :, :half])
    halve(bit, keep_far, got_far, keep_out.at[:, :, half:], send_out.at[:, :, half:])


def local(
    layer_input,
    value_proj,
    conv_taps,
    conv_pre,
    state_in,
    state_out,
    step_size,
    log_decay,
    skip_gain,
    grad_out,
):
    length, width = grad_out.shape
    heads = step_size.shape[0]
    state_width = state_in.shape[1]
    count = length // BLOCK
    features = layer_input.shape[1]
    spans_of = lax.axis_size("context")
    members = lax.axis_size("tensor")

    layers = [layer_input]
    stride = members // 2
    while stride:
        layers += [swap(layer, "tensor", stride, 2, 1) for layer in layers]
        stride //= 2
    bits = members.bit_length() - 1
    layers = [layers[int(format(hop, f"0{bits}b")[::-1], 2)] for hop in range(members)]

    fetched = [grad_out, state_out, log_decay, state_in, step_size, conv_pre, conv_taps, layer_input]
    payload, states, grad_here, output_here, decay_here, input_here, step_here, pre_here, taps_here, layer_here = call(
        functools.partial(state_body, heads, len(fetched) - 3),
        [((state_width + PAD, width), BF16), ((count, state_width + ROW, width), F32)]
        + [(a.shape, a.dtype) for a in fetched],
        fetched,
        hbm=len(fetched),
        scratch=[pltpu.SemaphoreType.DMA((len(fetched),))],
        flops=2 * length * width * state_width,
        moved=2 * length * width,
        vmem=12,
    )

    base, coef = call(
        functools.partial(within_body, heads),
        [((length, width), F32), ((length, width), F32)],
        [skip_gain, input_here, output_here, grad_here, step_here, decay_here, pre_here],
        scalars=1,
        flops=64 * length * width * BLOCK * 8,
        moved=12 * length * width,
        vmem=16,
    )

    stages = radices(spans_of, 4)
    stride, held = 1, []
    for radix in stages:
        last = stride * radix == spans_of
        received = [swap(payload, "context", stride, radix, hop, last) for hop in range(1, radix)]
        if not last:
            following = stages[stages.index(radix) + 1] if len(stages) == 2 else 4
            rows = state_width if following == 2 else state_width + PAD
            payload, *held = call(
                functools.partial(merge_body, radix, stride, not held),
                [((rows, width), BF16), ((state_width + ROW, width), F32)],
                [payload, *received, *held, base],
                idle=1,
            )
            stride *= radix

    turned, ends = call(
        functools.partial(turn_body, members),
        [((members * features, length), BF16), ((members, PAD, features), BF16)],
        [layer_here, *layers[1:]],
        moved=2 * members * features * length,
    )
    ends = lax.ppermute(ends, "context", [(i, i + 1) for i in range(spans_of - 1)])

    total_rows = members * features
    chunk = total_rows // spans_of
    scaling = 1.0 / math.sqrt(length * spans_of)
    split_shape = (spans_of // 2, chunk, width // 2)
    send_near, send_far, grads, turned_ends = call(
        functools.partial(tail_body, stages[-1], stride, not held, members, chunk),
        [(split_shape, BF16), (split_shape, BF16), ((PAD + length, width), BF16), ((total_rows, PAD), BF16)],
        [*received, *held, states, base, coef, input_here, taps_here, ends, turned],
        scratch=[pltpu.VMEM((length + 2 * PAD, width), F32)],
        flops=2 * length * width * total_rows,
        moved=16 * length * width,
        vmem=16,
    )
    keep_near, keep_far = call(
        functools.partial(kept_body, chunk),
        [(split_shape, F32), (split_shape, F32)],
        [turned, turned_ends, grads],
        flops=length * width * total_rows,
        moved=8 * length * width,
    )

    got_near = swap(send_near, "context", 1, 2, 1)
    got_far = swap(send_far, "context", 2, 2, 1)

    quarter_shape = (spans_of // 4, chunk, width // 2)
    keep_near, send_near, keep_far, send_far = call(
        halve_both_body,
        [(quarter_shape, F32), (quarter_shape, BF16)] * 2,
        [keep_near, got_near, keep_far, got_far],
        moved=2 * total_rows * width,
        vmem=8,
    )
    got_near = swap(send_near, "context", 2, 2, 1)
    got_far = swap(send_far, "context", 1, 2, 1)
    half = members // 2
    high = PAD + length
    size = -(-half * high // (3 * PAD)) * PAD
    sizes = [min(size, half * high - start) for start in range(0, half * high, size)]
    shares = call(
        functools.partial(share_body, members, sizes),
        [((high, features), F32)] * half + [((size, features), BF16) for size in sizes],
        [grads, value_proj],
        flops=2 * length * width * total_rows,
        moved=8 * length * width,
        vmem=12,
    )
    stride = 1
    share, arrived = shares[:half], [swap(a, "tensor", stride, 2, 1) for a in shares[half:]]
    while half > 1:
        count, half = half, half // 2
        outs = call(
            functools.partial(share_sum_body, count, sizes),
            [((high, features), F32)] * half + [((high, features), BF16)] * half,
            [*share, *arrived],
            moved=4 * length * features,
        )
        stride *= 2
        sizes = [high] * half
        share, arrived = outs[:half], [swap(a, "tensor", stride, 2, 1) for a in outs[half:]]

    joined_shape = (spans_of // 8, chunk, width)
    keep, send = call(
        join_body,
        [(joined_shape, F32), (joined_shape, BF16)],
        [keep_near, got_near, keep_far, got_far],
        moved=total_rows * width,
        vmem=8,
    )
    got, shift = swap(send, "context", 4, 2, 1), 3
    while keep.shape[0] > 1:
        joined_shape = (keep.shape[0] // 2, chunk, width)
        keep, send = call(
            functools.partial(halve_body, shift),
            [(joined_shape, F32), (joined_shape, BF16)],
            [keep, got],
            moved=total_rows * width,
            vmem=8,
        )
        got = swap(send, "context", 1 << shift, 2, 1)
        shift += 1
    head, own = call(
        settle_body,
        [((PAD, features), F32), ((length, features), F32)],
        [*share, *arrived],
    )
    ahead = lax.ppermute(head, "context", [(i + 1, i) for i in range(spans_of - 1)])
    grad_value_proj, grad_input = call(
        functools.partial(end_body, scaling),
        [((chunk, width), F32), ((length, features), BF16)],
        [keep, got, own, ahead],
    )
    return (grad_input, grad_value_proj)


def solution(mesh):
    return jax.shard_map(
        local,
        mesh=mesh,
        in_specs=(
            P("context", "tensor"),
            P(None, "tensor"),
            P(None, "tensor"),
            P("context", "tensor"),
            P("context", None),
            P("context", None),
            P("tensor", "context"),
            P("tensor", "context"),
            P("tensor"),
            P("context", "tensor"),
        ),
        out_specs=(P("context", "tensor"), P("context", "tensor")),
        check_vma=False,
    )
```

```python
import functools
import math

import jax
import jax.numpy as jnp
from jax import lax
from jax.experimental import pallas as pl
from jax.experimental.pallas import tpu as pltpu
from jax.sharding import PartitionSpec as P

CONV = 4
BLOCK = 256
PAD = 16
ROW = 8
F32 = jnp.float32
BF16 = jnp.bfloat16
MIB = 1024 * 1024


def call(body, out_shapes, operands, scalars=0, hbm=0, idle=0, scratch=(), flops=0, moved=0, vmem=8):
    blocks = len(operands) - scalars - hbm - idle
    in_specs = [pl.BlockSpec(memory_space=pltpu.SMEM)] * scalars
    in_specs += [pl.BlockSpec(memory_space=pltpu.VMEM)] * blocks
    in_specs += [pl.BlockSpec(memory_space=pltpu.HBM)] * hbm
    in_specs += [pl.BlockSpec(memory_space=pl.ANY)] * idle
    kept = len(operands) - idle

    def run(*refs):
        body(*refs[:kept], *refs[len(operands) :])

    operands = list(operands)
    for index in range(scalars + blocks, scalars + blocks + hbm):
        operands[index] = pltpu.with_memory_space_constraint(operands[index], pltpu.HBM)
    return pl.pallas_call(
        run,
        out_shape=[jax.ShapeDtypeStruct(shape, kind) for shape, kind in out_shapes],
        in_specs=in_specs,
        out_specs=[pl.BlockSpec(memory_space=pltpu.VMEM)] * len(out_shapes),
        scratch_shapes=list(scratch),
        compiler_params=pltpu.CompilerParams(vmem_limit_bytes=vmem * MIB),
        cost_estimate=pl.CostEstimate(flops=flops, bytes_accessed=moved, transcendentals=0),
    )(*operands)


def radices(count, largest):
    found = []
    while count > 1:
        radix = next(r for r in range(min(largest, count), count + 1) if count % r == 0)
        found.append(radix)
        count //= radix
    return found


def partner(digit, radix, hop):
    if radix & (radix - 1) == 0:
        return digit ^ hop
    return (digit + hop) % radix


def origin(digit, radix, hop):
    if radix & (radix - 1) == 0:
        return digit ^ hop
    return (digit + radix - hop) % radix


def swap(value, axis, stride, radix, hop, back=False):
    count = lax.axis_size(axis)
    pairs = []
    for source in range(count):
        digit = source // stride % radix
        target = source + (partner(digit, radix, hop) - digit) * stride
        if not back or target < source:
            pairs.append((source, target))
    return lax.ppermute(value, axis, pairs)


def dot(a, b, contract):
    return lax.dot_general(a, b, ((contract[:1], contract[1:]), ((), ())), preferred_element_type=F32)


def spread_heads(heads, width):
    lane = lax.broadcasted_iota(jnp.int32, (heads, width), 1)
    head = lax.broadcasted_iota(jnp.int32, (heads, width), 0)
    return (lane // (width // heads) == head).astype(F32)


def spread_scalars(ref, heads, width):
    head = lax.broadcasted_iota(jnp.int32, (1, width), 1) // (width // heads)
    wide = jnp.zeros((1, width), F32)
    for index in range(heads):
        wide = jnp.where(head == index, ref[index], wide)
    return wide


def widen(per_head, spreader):
    high = per_head.astype(BF16).astype(F32)
    parts = jnp.concatenate([high, per_head - high], axis=0).astype(BF16)
    twice = jnp.concatenate([spreader, spreader], axis=0).astype(BF16)
    return dot(parts, twice, (0, 0))


def split(values):
    high = values.astype(BF16).astype(F32)
    middle = (values - high).astype(BF16).astype(F32)
    return high, middle, values - high - middle


def running(decay_blk):
    heads, length = decay_blk.shape
    row = lax.broadcasted_iota(jnp.int32, (length, length), 0)
    column = lax.broadcasted_iota(jnp.int32, (length, length), 1)
    parts = jnp.concatenate(split(decay_blk), axis=0).astype(BF16)
    sums = dot(parts, (row <= column).astype(F32).astype(BF16), (1, 0))
    return sums[:heads] + (sums[heads : 2 * heads] + sums[2 * heads :])


def pack_state(ref, state, decay_row):
    rows = state.shape[0]
    ref[:rows, :] = state.astype(BF16)
    high, middle, low = split(decay_row)
    place = lax.broadcasted_iota(jnp.int32, (PAD, decay_row.shape[1]), 0)
    packed = jnp.where(place == 0, high, jnp.where(place == 1, middle, jnp.where(place == 2, low, 0.0)))
    ref[rows:, :] = packed.astype(BF16)


def unpack_state(ref):
    rows = ref.shape[0] - PAD
    return ref[:rows, :].astype(F32), jnp.sum(ref[rows:, :].astype(F32), axis=0, keepdims=True)


def later_sum(digit, places, states, decays):
    total = None
    span = jnp.zeros_like(decays[0])
    for index, place in enumerate(places):
        between = jnp.zeros_like(decays[0])
        for other, other_place in enumerate(places):
            if other != index:
                inside = jnp.logical_and(other_place > digit, other_place < place)
                between = between + jnp.where(inside, decays[other], 0.0)
        weight = jnp.where(place > digit, jnp.exp(between), 0.0)
        total = weight * states[index] if total is None else total + weight * states[index]
        span = span + jnp.where(place > digit, decays[index], 0.0)
    return total, span


def state_body(heads, others, grad_hbm, output_hbm, decay_hbm, *refs):
    rest, refs = refs[:others], refs[others:]
    payload_ref, states_ref, grad_ref, output_ref, decay_ref = refs[:5]
    rest_out, sems = refs[5:-1], refs[-1]
    blocks = [slice(k * BLOCK, (k + 1) * BLOCK) for k in range(grad_ref.shape[0] // BLOCK)]
    pairs = [(decay_hbm, decay_ref), (output_hbm, output_ref)]
    pairs += [(grad_hbm.at[rows, :], grad_ref.at[rows, :]) for rows in blocks]
    pairs += list(zip(rest, rest_out))
    copies = [pltpu.make_async_copy(a, b, sems.at[index]) for index, (a, b) in enumerate(pairs)]
    for copy in copies:
        copy.start()
    copies[0].wait()
    width = grad_ref.shape[1]
    count = grad_ref.shape[0] // BLOCK
    spreader = spread_heads(heads, width)
    sums = [running(decay_ref[:, rows]) for rows in blocks]
    factors = [widen(jnp.exp(cumulative), spreader) for cumulative in sums]
    spans = [jnp.sum(spreader * cumulative[:, BLOCK - 1 :], axis=0, keepdims=True) for cumulative in sums]
    copies[1].wait()
    states = []
    for k, rows in enumerate(blocks):
        copies[2 + k].wait()
        weighted = (grad_ref[rows, :].astype(F32) * factors[k]).astype(BF16)
        states.append(dot(output_ref[rows, :], weighted, (0, 0)))
    total, span = states[-1], spans[-1]
    for k in reversed(range(count - 1)):
        total = states[k] + jnp.exp(spans[k]) * total
        span = span + spans[k]
    pack_state(payload_ref, total, span)
    for k in range(count):
        keep_state(states_ref.at[k], states[k], spans[k])
    for copy in copies[2 + count :]:
        copy.wait()


def keep_state(ref, state, span):
    rows = state.shape[0]
    ref[:rows, :] = state
    ref[rows:, :] = jnp.broadcast_to(span, (ROW, span.shape[1]))


def kept_state(ref):
    rows = ref.shape[0] - ROW
    return ref[:rows, :], ref[rows : rows + 1, :]


def merge_body(radix, stride, first, payload_ref, *refs):
    received = refs[: radix - 1]
    next_ref, held_out = refs[-2:]
    digit = lax.axis_index("context") // stride % radix
    pairs = [unpack_state(ref) for ref in (payload_ref, *received)]
    states, decays = [a for a, _ in pairs], [b for _, b in pairs]
    places = [origin(digit, radix, hop) for hop in range(radix)]
    whole, whole_span = later_sum(-1, places, states, decays)
    if next_ref.shape[0] > whole.shape[0]:
        pack_state(next_ref, whole, whole_span)
    else:
        next_ref[...] = whole.astype(BF16)
    later, span = later_sum(digit, places[1:], states[1:], decays[1:])
    if not first:
        held, reach = kept_state(refs[radix - 1])
        later = held + jnp.exp(reach) * later
        span = reach + span
    keep_state(held_out, later, span)


def within_body(heads, skip_ref, *refs):
    input_ref, output_ref, grad_ref, step_ref, decay_ref, pre_ref, base_ref, coef_ref = refs
    for k in range(grad_ref.shape[0] // BLOCK):
        rows = slice(k * BLOCK, (k + 1) * BLOCK)
        within_block(
            heads,
            skip_ref,
            *(ref.at[rows, :] for ref in (input_ref, output_ref, grad_ref)),
            *(ref.at[:, rows] for ref in (step_ref, decay_ref)),
            *(ref.at[rows, :] for ref in (pre_ref, base_ref, coef_ref)),
        )


def within_block(heads, skip_ref, input_ref, output_ref, grad_ref, step_ref, decay_ref, pre_ref, base_ref, coef_ref):
    width = grad_ref.shape[1]
    head_width = width // heads
    group = max(1, 128 // head_width)
    half = BLOCK // 2
    spreader = spread_heads(heads, width)
    cumulative = running(decay_ref[...])
    across = cumulative.T
    scores = dot(input_ref[...], output_ref[...], (1, 1))
    step = step_ref[...]
    step_wide = widen(step, spreader)
    reach_wide = widen(step * jnp.exp(cumulative[:, BLOCK - 1 :] - cumulative), spreader)
    skip_wide = spread_scalars(skip_ref, heads, width)
    row = lax.broadcasted_iota(jnp.int32, (half, half), 0)
    column = lax.broadcasted_iota(jnp.int32, (half, half), 1)
    keep = column >= row
    lane = lax.broadcasted_iota(jnp.int32, (half, group * head_width), 1) // head_width

    def weigh(head, rows, columns, diagonal):
        spread = cumulative[head : head + 1, columns] - across[rows, head : head + 1]
        if diagonal:
            spread = jnp.where(keep, spread, -jnp.inf)
        return (scores[rows, columns] * jnp.exp(spread)).astype(BF16)

    first, second = slice(0, half), slice(half, BLOCK)
    for start in range(0, heads, group):
        channels = slice(start * head_width, (start + group) * head_width)
        grads = grad_ref[:, channels]
        upper = lower = None
        for member in range(group):
            head = start + member
            top = jnp.concatenate([weigh(head, first, first, True), weigh(head, first, second, False)], axis=1)
            one = dot(top, grads, (1, 0))
            two = dot(weigh(head, second, second, True), grads[half:, :], (1, 0))
            upper = one if upper is None else jnp.where(lane == member, one, upper)
            lower = two if lower is None else jnp.where(lane == member, two, lower)
        for rows, product in ((first, upper), (second, lower)):
            pre = pre_ref[rows, channels].astype(F32)
            gate = 1.0 / (1.0 + jnp.exp(-pre))
            slope = gate * (1.0 + pre * (1.0 - gate))
            direct = step_wide[rows, channels] * product + skip_wide[:, channels] * grads[rows, :].astype(F32)
            base_ref[rows, channels] = slope * direct
            coef_ref[rows, channels] = slope * reach_wide[rows, channels]


def turn_body(members, *refs):
    pieces, turned_ref, ends_ref = refs[:members], refs[members], refs[-1]
    length, features = pieces[0].shape
    for hop in range(members):
        source = origin(lax.axis_index("tensor"), members, hop)
        ends_ref[source] = pieces[hop][length - PAD :, :]
        start = pl.multiple_of(source * features, features)
        turned_ref[pl.ds(start, features), :] = pieces[hop][...].T


def tail_body(radix, stride, first, members, chunk, *refs):
    received, refs = refs[: radix - 1], refs[radix - 1 :]
    if not first:
        held_ref, refs = refs[0], refs[1:]
    states_ref, base_ref, coef_ref, input_ref, taps_ref, ends_ref, layer_ref = refs[:7]
    send_near, send_far, grads_ref, turned_ref, conv_ref = refs[7:]
    length, width = base_ref.shape
    place = lax.axis_index("context")
    digit = place // stride % radix
    if radix == 2:
        carry = jnp.where(digit == 0, received[0][...].astype(F32), 0.0)
    else:
        pairs = [unpack_state(ref) for ref in received]
        places = [origin(digit, radix, hop) for hop in range(1, radix)]
        carry, _ = later_sum(digit, places, [a for a, _ in pairs], [b for _, b in pairs])
    if not first:
        held, reach = kept_state(held_ref)
        carry = held + jnp.exp(reach) * carry
    conv_ref[:PAD, :] = jnp.zeros((PAD, width), F32)
    conv_ref[PAD + length :, :] = jnp.zeros((PAD, width), F32)
    for k in reversed(range(length // BLOCK)):
        rows = slice(k * BLOCK, (k + 1) * BLOCK)
        product = dot(input_ref[rows, :], carry.astype(BF16), (1, 0))
        value = base_ref[rows, :] + coef_ref[rows, :] * product
        conv_ref[PAD + k * BLOCK : PAD + (k + 1) * BLOCK, :] = value.astype(BF16).astype(F32)
        if k:
            state, span = kept_state(states_ref.at[k])
            carry = state + jnp.exp(span) * carry
    total = None
    for offset in range(CONV):
        shift = CONV - 1 - offset
        term = taps_ref[offset : offset + 1, :] * conv_ref[shift : shift + PAD + length, :]
        total = term if total is None else total + term
    grads_ref[...] = total.astype(BF16)
    features = ends_ref.shape[2]
    for index in range(members):
        turned_ref[index * features : (index + 1) * features, :] = ends_ref[index].T
    products(chunk, 1, layer_ref, turned_ref, grads_ref, send_near, send_far)


def products(chunk, flip, layer_ref, turned_ref, grads_ref, near_ref, far_ref):
    place = lax.axis_index("context")
    near_bit, far_bit = (place & 1) ^ flip, ((place >> 1) & 1) ^ flip
    half = near_ref.shape[2]
    for channels, out_ref, number in (
        (slice(0, half), near_ref, lambda i: 2 * i + near_bit),
        (slice(half, 2 * half), far_ref, lambda i: (i & 1) + ((i >> 1) << 2) + 2 * far_bit),
    ):
        starts = [pl.multiple_of(number(i) * chunk, chunk) for i in range(out_ref.shape[0])]
        layers = jnp.concatenate([layer_ref[pl.ds(start, chunk), :] for start in starts], axis=0)
        ends = jnp.concatenate([turned_ref[pl.ds(start, chunk), :] for start in starts], axis=0)
        product = dot(layers, grads_ref[PAD:, channels], (1, 0)) + dot(ends, grads_ref[:PAD, channels], (1, 0))
        for i in range(out_ref.shape[0]):
            out_ref[i] = product[i * chunk : (i + 1) * chunk, :].astype(out_ref.dtype)


def kept_body(chunk, layer_ref, turned_ref, grads_ref, keep_near, keep_far):
    products(chunk, 0, layer_ref, turned_ref, grads_ref, keep_near, keep_far)


def overlaps(index, high, sizes):
    start, found = 0, []
    for part, size in enumerate(sizes):
        first, last = max(start, index * high), min(start + size, (index + 1) * high)
        if first < last:
            found.append((part, slice(first - start, last - start), slice(first - index * high, last - index * high)))
        start += size
    return found


def share_body(members, sizes, grads_ref, proj_ref, *refs):
    keep_refs, send_refs = refs[: members // 2], refs[members // 2 :]
    high, features = keep_refs[0].shape
    for hop in range(members):
        goal = lax.axis_index("tensor") ^ hop
        block = proj_ref[pl.ds(pl.multiple_of(goal * features, features), features), :]
        share = dot(grads_ref[...], block, (1, 1))
        if hop % 2:
            for part, there, here in overlaps(hop // 2, high, sizes):
                send_refs[part][there, :] = share[here, :].astype(BF16)
        else:
            keep_refs[hop // 2][...] = share


def share_sum_body(count, sizes, *refs):
    keeps, arrivals, outs = refs[:count], refs[count : count + len(sizes)], refs[count + len(sizes) :]
    for index in range(count):
        out = outs[index // 2 + index % 2 * (count // 2)]
        for part, there, here in overlaps(index, out.shape[0], sizes):
            out[here, :] = (keeps[index][here, :] + arrivals[part][there, :].astype(F32)).astype(out.dtype)


def settle_body(share_ref, arrived_ref, head_ref, own_ref):
    head_ref[...] = share_ref[:PAD, :] + arrived_ref[:PAD, :].astype(F32)
    own_ref[...] = share_ref[PAD:, :] + arrived_ref[PAD:, :].astype(F32)


def end_body(scaling, keep_ref, got_ref, own_ref, ahead_ref, proj_out, input_out):
    proj_out[...] = (keep_ref[0] + got_ref[0].astype(F32)) * scaling
    rest = own_ref.shape[0] - PAD
    input_out[:rest, :] = own_ref[:rest, :].astype(BF16)
    input_out[rest:, :] = (own_ref[rest:, :] + ahead_ref[...]).astype(BF16)


def halve(bit, keep_ref, received_ref, keep_out, send_out):
    for index in range(keep_out.shape[0]):
        mine, other = 2 * index + bit, 2 * index + 1 - bit
        keep_out[index] = keep_ref[mine] + received_ref[mine].astype(F32)
        send_out[index] = (keep_ref[other] + received_ref[other].astype(F32)).astype(BF16)


def bit_of_place(shift):
    return (lax.axis_index("context") >> shift) & 1


def halve_body(shift, keep_ref, received_ref, keep_out, send_out):
    halve(bit_of_place(shift), keep_ref, received_ref, keep_out, send_out)


def halve_both_body(keep_near, got_near, keep_far, got_far, near_out, near_send, far_out, far_send):
    halve(bit_of_place(1), keep_near, got_near, near_out, near_send)
    halve(bit_of_place(0), keep_far, got_far, far_out, far_send)


def join_body(keep_near, got_near, keep_far, got_far, keep_out, send_out):
    bit = bit_of_place(2)
    half = keep_near.shape[2]
    halve(bit, keep_near, got_near, keep_out.at[:, :, :half], send_out.at[:, :, :half])
    halve(bit, keep_far, got_far, keep_out.at[:, :, half:], send_out.at[:, :, half:])


def local(
    layer_input,
    value_proj,
    conv_taps,
    conv_pre,
    state_in,
    state_out,
    step_size,
    log_decay,
    skip_gain,
    grad_out,
):
    length, width = grad_out.shape
    heads = step_size.shape[0]
    state_width = state_in.shape[1]
    count = length // BLOCK
    features = layer_input.shape[1]
    spans_of = lax.axis_size("context")
    members = lax.axis_size("tensor")

    layers = [layer_input]
    stride = members // 2
    while stride:
        layers += [swap(layer, "tensor", stride, 2, 1) for layer in layers]
        stride //= 2
    bits = members.bit_length() - 1
    layers = [layers[int(format(hop, f"0{bits}b")[::-1], 2)] for hop in range(members)]

    fetched = [grad_out, state_out, log_decay, state_in, step_size, conv_pre, conv_taps]
    payload, states, grad_here, output_here, decay_here, input_here, step_here, pre_here, taps_here = call(
        functools.partial(state_body, heads, len(fetched) - 3),
        [((state_width + PAD, width), BF16), ((count, state_width + ROW, width), F32)]
        + [(a.shape, a.dtype) for a in fetched],
        fetched,
        hbm=len(fetched),
        scratch=[pltpu.SemaphoreType.DMA((len(fetched) - 1 + count,))],
        flops=2 * length * width * state_width,
        moved=2 * length * width,
        vmem=12,
    )

    base, coef = call(
        functools.partial(within_body, heads),
        [((length, width), F32), ((length, width), F32)],
        [skip_gain, input_here, output_here, grad_here, step_here, decay_here, pre_here],
        scalars=1,
        flops=64 * length * width * BLOCK * 8,
        moved=12 * length * width,
        vmem=16,
    )

    stages = radices(spans_of, 4)
    stride, held = 1, []
    for radix in stages:
        last = stride * radix == spans_of
        received = [swap(payload, "context", stride, radix, hop, last) for hop in range(1, radix)]
        if not last:
            following = stages[stages.index(radix) + 1] if len(stages) == 2 else 4
            rows = state_width if following == 2 else state_width + PAD
            payload, *held = call(
                functools.partial(merge_body, radix, stride, not held),
                [((rows, width), BF16), ((state_width + ROW, width), F32)],
                [payload, *received, *held, base],
                idle=1,
            )
            stride *= radix

    turned, ends = call(
        functools.partial(turn_body, members),
        [((members * features, length), BF16), ((members, PAD, features), BF16)],
        layers,
        moved=2 * members * features * length,
    )
    ends = lax.ppermute(ends, "context", [(i, i + 1) for i in range(spans_of - 1)])

    total_rows = members * features
    chunk = total_rows // spans_of
    scaling = 1.0 / math.sqrt(length * spans_of)
    split_shape = (spans_of // 2, chunk, width // 2)
    send_near, send_far, grads, turned_ends = call(
        functools.partial(tail_body, stages[-1], stride, not held, members, chunk),
        [(split_shape, BF16), (split_shape, BF16), ((PAD + length, width), BF16), ((total_rows, PAD), BF16)],
        [*received, *held, states, base, coef, input_here, taps_here, ends, turned],
        scratch=[pltpu.VMEM((length + 2 * PAD, width), F32)],
        flops=2 * length * width * total_rows,
        moved=16 * length * width,
        vmem=16,
    )
    keep_near, keep_far = call(
        functools.partial(kept_body, chunk),
        [(split_shape, F32), (split_shape, F32)],
        [turned, turned_ends, grads],
        flops=length * width * total_rows,
        moved=8 * length * width,
    )

    got_near = swap(send_near, "context", 1, 2, 1)
    got_far = swap(send_far, "context", 2, 2, 1)

    quarter_shape = (spans_of // 4, chunk, width // 2)
    keep_near, send_near, keep_far, send_far = call(
        halve_both_body,
        [(quarter_shape, F32), (quarter_shape, BF16)] * 2,
        [keep_near, got_near, keep_far, got_far],
        moved=2 * total_rows * width,
        vmem=8,
    )
    got_near = swap(send_near, "context", 2, 2, 1)
    got_far = swap(send_far, "context", 1, 2, 1)
    half = members // 2
    high = PAD + length
    size = -(-half * high // (3 * PAD)) * PAD
    sizes = [min(size, half * high - start) for start in range(0, half * high, size)]
    shares = call(
        functools.partial(share_body, members, sizes),
        [((high, features), F32)] * half + [((size, features), BF16) for size in sizes],
        [grads, value_proj],
        flops=2 * length * width * total_rows,
        moved=8 * length * width,
        vmem=12,
    )
    stride = 1
    share, arrived = shares[:half], [swap(a, "tensor", stride, 2, 1) for a in shares[half:]]
    while half > 1:
        count, half = half, half // 2
        outs = call(
            functools.partial(share_sum_body, count, sizes),
            [((high, features), F32)] * half + [((high, features), BF16)] * half,
            [*share, *arrived],
            moved=4 * length * features,
        )
        stride *= 2
        sizes = [high] * half
        share, arrived = outs[:half], [swap(a, "tensor", stride, 2, 1) for a in outs[half:]]

    joined_shape = (spans_of // 8, chunk, width)
    keep, send = call(
        join_body,
        [(joined_shape, F32), (joined_shape, BF16)],
        [keep_near, got_near, keep_far, got_far],
        moved=total_rows * width,
        vmem=8,
    )
    got, shift = swap(send, "context", 4, 2, 1), 3
    while keep.shape[0] > 1:
        joined_shape = (keep.shape[0] // 2, chunk, width)
        keep, send = call(
            functools.partial(halve_body, shift),
            [(joined_shape, F32), (joined_shape, BF16)],
            [keep, got],
            moved=total_rows * width,
            vmem=8,
        )
        got = swap(send, "context", 1 << shift, 2, 1)
        shift += 1
    head, own = call(
        settle_body,
        [((PAD, features), F32), ((length, features), F32)],
        [*share, *arrived],
    )
    ahead = lax.ppermute(head, "context", [(i + 1, i) for i in range(spans_of - 1)])
    grad_value_proj, grad_input = call(
        functools.partial(end_body, scaling),
        [((chunk, width), F32), ((length, features), BF16)],
        [keep, got, own, ahead],
    )
    return (grad_input, grad_value_proj)


def solution(mesh):
    return jax.shard_map(
        local,
        mesh=mesh,
        in_specs=(
            P("context", "tensor"),
            P(None, "tensor"),
            P(None, "tensor"),
            P("context", "tensor"),
            P("context", None),
            P("context", None),
            P("tensor", "context"),
            P("tensor", "context"),
            P("tensor"),
            P("context", "tensor"),
        ),
        out_specs=(P("context", "tensor"), P("context", "tensor")),
        check_vma=False,
    )
```
